512 devices in a mesh: dp: 64 (over x, z), mp: 8 (over y, core).
Axes of the slice: x: 4, y: 4, z: 16, core: 2. Of those that a mesh axis runs over, the one named last changes fastest.
Arguments:
- queries: bfloat16 [65536, 2048], P(('dp', 'mp')), may hold values from -8 to 8
- encoder_keys: bfloat16 [73728, 2048], P('dp', 'mp'), may hold values from -8 to 8
- encoder_values: bfloat16 [73728, 2048], P('dp', 'mp'), may hold values from -6 to 6
- context_grad: bfloat16 [65536, 2048], P(('dp', 'mp')), may hold values from -6 to 6
- encoder_lengths: int32 [64, 2], replicated, may hold values from 288 to 576, as said below
- decoder_lengths: int32 [64, 2], replicated, may hold values from 128 to 512, as said below
- target_device: int32 [64, 2], replicated, may hold values from 0 to 63, as said below
Outputs:
- context: bfloat16 [65536, 2048], P(('dp', 'mp'))
- query_grad: bfloat16 [65536, 2048], P(('dp', 'mp'))
- key_grad: bfloat16 [73728, 2048], P('dp', 'mp')
- value_grad: bfloat16 [73728, 2048], P('dp', 'mp')
The draws below stay inside these ranges and needn't reach their ends.
Inputs may be any that keep to these rules, and one draw needn't show every extreme that they name: target_device[a, k] = (a + s_k) mod 64 with one shift s_k for each column; the shifts are 1 or more and add up to 63. `encoder_lengths`: each row has an entry equal to 576. `decoder_lengths`: each row has an entry equal to 512.
All inputs are finite; a program needn't handle non-finite values.
Results may differ from the reference program's by a relative error of at most 0.011.
Values may be sent and summed in bfloat16 or wider, within the bound.
No kernel may reach another device: no remote copies, remote signals or barrier semaphores. Data moves between devices by JAX's collectives and lax.ppermute only.
A program may use at most 64 MiB of HBM per device.

```python
import jax
import jax.numpy as jnp
from jax import lax

HEAD_DIM = 256
SEQ_DEV = 2
CAP = 576
TCAP = 512
ATTN_WIDTH = 2048
OWNERS = 64
E_DEV = 1152
T_DEV = 1024
ENC_TOK = 73728
DEC_TOK = 65536


def draw_encoder_keys(key, part):
    key = jax.random.fold_in(key, 1)
    noise_key, scale_key = jax.random.split(key)
    noise = jax.random.normal(noise_key, (ENC_TOK, ATTN_WIDTH), jnp.float32)
    scales = jnp.exp(jax.random.uniform(scale_key, (ENC_TOK, 1), jnp.float32, jnp.log(0.3), jnp.log(3.0)))
    values = noise * scales
    return jnp.clip(values, -8.0, 8.0).astype(jnp.bfloat16)


def draw_queries(key, part):
    key = jax.random.fold_in(key, 2)
    noise_key, scale_key = jax.random.split(key, 2)
    noise = jax.random.normal(noise_key, (DEC_TOK, ATTN_WIDTH), jnp.float32)
    scales = jnp.exp(jax.random.uniform(scale_key, (DEC_TOK, 1), jnp.float32, jnp.log(0.3), jnp.log(3.0)))
    values = noise * scales
    return jnp.clip(values, -8.0, 8.0).astype(jnp.bfloat16)


def draw_target_device(key, part):
    key = jax.random.fold_in(key, 3)
    first = jax.random.randint(key, (1,), 1, OWNERS - 1).astype(jnp.int32)
    shifts = jnp.concatenate([first, OWNERS - 1 - first]).astype(jnp.int32)
    rows = jnp.arange(OWNERS, dtype=jnp.int32)
    return ((rows[:, None] + shifts[None, :]) % OWNERS).astype(jnp.int32)


def draw_encoder_lengths(key, part):
    key = jax.random.fold_in(key, 4)
    value_key, full_key = jax.random.split(key)
    values = jax.random.randint(value_key, (OWNERS, SEQ_DEV), CAP // 2, CAP + 1).astype(jnp.int32)
    full = jax.random.randint(full_key, (OWNERS, 1), 0, SEQ_DEV).astype(jnp.int32)
    columns = jnp.arange(SEQ_DEV, dtype=jnp.int32)
    return jnp.where(columns[None, :] == full, CAP, values).astype(jnp.int32)


def draw_decoder_lengths(key, part):
    key = jax.random.fold_in(key, 5)
    value_key, full_key = jax.random.split(key)
    values = jax.random.randint(value_key, (OWNERS, SEQ_DEV), TCAP // 4, TCAP + 1).astype(jnp.int32)
    full = jax.random.randint(full_key, (OWNERS, 1), 0, SEQ_DEV).astype(jnp.int32)
    columns = jnp.arange(SEQ_DEV, dtype=jnp.int32)
    return jnp.where(columns[None, :] == full, TCAP, values).astype(jnp.int32)


def block_scale(own_key, shape, cuts, low, top_value):
    factor_of, own = 1.0, jax.random.fold_in(own_key, 6)
    for dim, shards_of in cuts:
        draws = jnp.exp(jax.random.uniform(jax.random.fold_in(own, dim), (shards_of,), jnp.float32, low / len(cuts), top_value / len(cuts)))
        factor_of = factor_of * jnp.repeat(draws, shape[dim] // shards_of).reshape([-1 if axis == dim else 1 for axis in range(len(shape))])
    return factor_of


def scatter_about(stream_key, extent, deviation, reach, cuts=(), held_as=jnp.bfloat16):
    values = deviation * jax.random.normal(stream_key, extent, jnp.float32)
    if cuts:
        values = values * block_scale(stream_key, extent, cuts, -0.22, 0.18)
    return jnp.clip(values, -reach, reach).astype(held_as)


def setup_inputs(seed: int = 0) -> dict:
    splits = jax.random.split(jax.random.key(seed), 8)
    queries = draw_queries(jax.random.fold_in(splits[7], 71), 0)
    encoder_keys = draw_encoder_keys(jax.random.fold_in(splits[7], 71), 0)
    encoder_values = scatter_about(splits[2], (ENC_TOK, ATTN_WIDTH), 1.0, 6.0, ((0, 64), (1, 8)))
    context_grad = scatter_about(splits[3], (DEC_TOK, ATTN_WIDTH), 1.0, 6.0, ((0, 512),))
    encoder_lengths = draw_encoder_lengths(jax.random.fold_in(splits[7], 71), 0)
    decoder_lengths = draw_decoder_lengths(jax.random.fold_in(splits[7], 71), 0)
    target_device = draw_target_device(jax.random.fold_in(splits[7], 71), 0)
    return dict(queries=queries, encoder_keys=encoder_keys, encoder_values=encoder_values, context_grad=context_grad, encoder_lengths=encoder_lengths, decoder_lengths=decoder_lengths, target_device=target_device)


def rounded(values):
    return lax.optimization_barrier(values.astype(jnp.bfloat16)).astype(jnp.float32)


def attend(query_slots, grad_slots, key_slots, value_slots, key_valid):
    seqs = query_slots.shape[0]
    query_count = query_slots.shape[1]
    key_count = key_slots.shape[1]
    width = query_slots.shape[2]
    head_count = width // HEAD_DIM
    scaling = HEAD_DIM ** -0.5
    query_heads = query_slots.astype(jnp.float32).reshape(seqs, query_count, head_count, HEAD_DIM)
    grad_heads = grad_slots.astype(jnp.float32).reshape(seqs, query_count, head_count, HEAD_DIM)
    key_heads = key_slots.astype(jnp.float32).reshape(seqs, key_count, head_count, HEAD_DIM)
    value_heads = value_slots.astype(jnp.float32).reshape(seqs, key_count, head_count, HEAD_DIM)
    scores = jnp.einsum("sthd,schd->shtc", query_heads, key_heads) * scaling
    scores = jnp.where(key_valid[:, None, None, :], scores, -1e30)
    row_max = jnp.max(scores, axis=3, keepdims=True)
    raised = jnp.exp(scores - row_max)
    probs = raised / jnp.sum(raised, axis=3, keepdims=True)
    probs_b = rounded(probs)
    context = jnp.einsum("shtc,schd->sthd", probs_b, value_heads).astype(jnp.bfloat16)
    prob_grad = jnp.einsum("sthd,schd->shtc", grad_heads, value_heads)
    row_dot = jnp.sum(probs * prob_grad, axis=3, keepdims=True)
    score_grad = rounded(probs * (prob_grad - row_dot))
    query_grad = (jnp.einsum("shtc,schd->sthd", score_grad, key_heads) * scaling).astype(jnp.bfloat16)
    key_grad = (jnp.einsum("shtc,sthd->schd", score_grad, query_heads) * scaling).astype(jnp.bfloat16)
    value_grad = jnp.einsum("shtc,sthd->schd", probs_b, grad_heads).astype(jnp.bfloat16)
    return (context.reshape(seqs * query_count, width), query_grad.reshape(seqs * query_count, width),
            key_grad.reshape(seqs * key_count, width), value_grad.reshape(seqs * key_count, width))


def reference(queries, encoder_keys, encoder_values, context_grad, encoder_lengths, decoder_lengths, target_device):
    owner_ids = jnp.arange(OWNERS, dtype=jnp.int32)
    hits = (target_device[:, None, :] == owner_ids[None, :, None]).astype(jnp.int32)
    sources = jnp.sum(owner_ids[:, None, None] * hits, axis=0).astype(jnp.int32)
    enc_starts = (jnp.cumsum(encoder_lengths, axis=1) - encoder_lengths).astype(jnp.int32)
    dec_starts = (jnp.cumsum(decoder_lengths, axis=1) - decoder_lengths).astype(jnp.int32)
    key_offsets = jnp.arange(CAP, dtype=jnp.int32)
    query_offsets = jnp.arange(TCAP, dtype=jnp.int32)

    def one_device(device, carry):
        context, query_grad, key_grad, value_grad = carry
        source_row = lax.dynamic_index_in_dim(sources, device, 0, keepdims=False)
        pick = (owner_ids[:, None] == source_row[None, :]).astype(jnp.int32)
        key_lengths = jnp.sum(encoder_lengths * pick, axis=0).astype(jnp.int32)
        key_starts = jnp.sum(enc_starts * pick, axis=0).astype(jnp.int32)
        key_valid = key_offsets[None, :] < key_lengths[:, None]
        key_index = jnp.where(key_valid, source_row[:, None] * E_DEV + key_starts[:, None] + key_offsets[None, :], 0)
        key_index = key_index.reshape(-1).astype(jnp.int32)
        key_slots = jnp.take(encoder_keys, key_index, axis=0).reshape(SEQ_DEV, CAP, ATTN_WIDTH)
        value_slots = jnp.take(encoder_values, key_index, axis=0).reshape(SEQ_DEV, CAP, ATTN_WIDTH)
        own_lengths = lax.dynamic_index_in_dim(decoder_lengths, device, 0, keepdims=False)
        own_starts = lax.dynamic_index_in_dim(dec_starts, device, 0, keepdims=False)
        query_valid = query_offsets[None, :] < own_lengths[:, None]
        query_index = jnp.where(query_valid, device * T_DEV + own_starts[:, None] + query_offsets[None, :], 0)
        query_index = query_index.reshape(-1).astype(jnp.int32)
        flat_valid = query_valid.reshape(-1)
        query_slots = jnp.where(flat_valid[:, None], jnp.take(queries, query_index, axis=0), jnp.zeros((), jnp.bfloat16))
        grad_slots = jnp.where(flat_valid[:, None], jnp.take(context_grad, query_index, axis=0), jnp.zeros((), jnp.bfloat16))
        ctx_slots, qgrad_slots, kgrad_slots, vgrad_slots = attend(
            query_slots.reshape(SEQ_DEV, TCAP, ATTN_WIDTH), grad_slots.reshape(SEQ_DEV, TCAP, ATTN_WIDTH),
            key_slots, value_slots, key_valid)
        dec_target = jnp.where(flat_valid, query_index, DEC_TOK).astype(jnp.int32)
        enc_target = jnp.where(key_valid.reshape(-1), key_index, ENC_TOK).astype(jnp.int32)
        context = context.at[dec_target].set(ctx_slots, mode="drop")
        query_grad = query_grad.at[dec_target].set(qgrad_slots, mode="drop")
        key_grad = key_grad.at[enc_target].set(kgrad_slots, mode="drop")
        value_grad = value_grad.at[enc_target].set(vgrad_slots, mode="drop")
        return context, query_grad, key_grad, value_grad

    start_carry = (jnp.zeros((DEC_TOK, ATTN_WIDTH), jnp.bfloat16), jnp.zeros((DEC_TOK, ATTN_WIDTH), jnp.bfloat16),
                   jnp.zeros((ENC_TOK, ATTN_WIDTH), jnp.bfloat16), jnp.zeros((ENC_TOK, ATTN_WIDTH), jnp.bfloat16))
    context, query_grad, key_grad, value_grad = lax.fori_loop(0, OWNERS, one_device, start_carry)
    return (context, query_grad, key_grad, value_grad)
```

```python
import functools

import jax
import jax.numpy as jnp
from jax import lax
from jax.experimental import pallas as pl
from jax.experimental.pallas import tpu as pltpu
from jax.sharding import PartitionSpec as P

HEAD_DIM = 256
SCALING = HEAD_DIM ** (-0.5)
WINDOW = 640
ROWS = 256
Z_LEN = 16
SMEM = pl.BlockSpec(memory_space=pltpu.SMEM)
NT = (((1,), (1,)), ((), ()))
TN = (((0,), (0,)), ((), ()))


def dot(a, b, dims=(((1,), (0,)), ((), ()))):
    return lax.dot_general(a, b, dims, preferred_element_type=jnp.float32)


def permuted(block, owners, moves):
    for move in moves:
        block = lax.ppermute(block, "dp", [(i, move(i) % owners) for i in range(owners)])
    return block


def shifted(block, owners, distance, around=0):
    if not around:
        return permuted(block, owners, [lambda i: i + distance])
    step = around * Z_LEN // 4

    def first(i):
        return i // Z_LEN * Z_LEN + (i + step) % Z_LEN

    inverse = {first(i): i for i in range(owners)}
    return permuted(block, owners, [first, lambda i: inverse[i] + distance])


def pack_kernel(scal, q_ref, g_ref, xa_ref, xb_ref):
    total = q_ref.shape[0]
    cap = xa_ref.shape[1]
    row = lax.broadcasted_iota(jnp.int32, (cap, total), 0)
    col = lax.broadcasted_iota(jnp.int32, (cap, total), 1)
    for n, x_ref in enumerate((xa_ref, xb_ref)):
        pick = ((col - row == scal[n]) & (row < scal[n + 2])).astype(jnp.float32).astype(jnp.bfloat16)
        x_ref[0] = dot(pick, q_ref[...]).astype(x_ref.dtype)
        x_ref[1] = dot(pick, g_ref[...]).astype(x_ref.dtype)


def merge_kernel(scal, ya_ref, yb_ref, ctx_ref, dq_ref):
    total = ctx_ref.shape[0]
    cap = ya_ref.shape[1]
    row = lax.broadcasted_iota(jnp.int32, (total, cap), 0)
    col = lax.broadcasted_iota(jnp.int32, (total, cap), 1)
    picks = [
        ((row - col == scal[n]) & (col < scal[n + 2])).astype(jnp.float32).astype(jnp.bfloat16)
        for n in range(2)
    ]
    for n, out_ref in enumerate((ctx_ref, dq_ref)):
        out_ref[...] = (dot(picks[0], ya_ref[n]) + dot(picks[1], yb_ref[n])).astype(out_ref.dtype)


def attend_kernel(last, scal, x_ref, k_ref, v_ref, *refs):
    if last:
        dk_in, dv_in, y_ref, dk_ref, dv_ref, acc_k, acc_v = refs
    else:
        y_ref, dk_ref, dv_ref, acc_k, acc_v = refs
    step = pl.program_id(0)
    start = pl.multiple_of(scal[0], 16)
    low, high, live = scal[1], scal[2], scal[3]
    keys = k_ref[pl.ds(start, WINDOW), :]
    values = v_ref[pl.ds(start, WINDOW), :]
    rows = x_ref.shape[1]
    valid = lax.broadcasted_iota(jnp.int32, (rows, 1), 0) + step * rows < live
    q = x_ref[0]
    g = x_ref[1]
    col = lax.broadcasted_iota(jnp.int32, (1, WINDOW), 1) + start
    scores = dot(q, keys, NT) * SCALING
    scores = jnp.where((col >= low) & (col < high), scores, -1e30)
    raised = jnp.exp(scores - jnp.max(scores, axis=1, keepdims=True))
    probs = raised * (1.0 / jnp.sum(raised, axis=1, keepdims=True))
    probs_b = probs.astype(jnp.bfloat16)
    prob_grad = dot(g, values, NT)
    row_dot = jnp.sum(probs * prob_grad, axis=1, keepdims=True)
    score_grad = (probs * (prob_grad - row_dot)).astype(jnp.bfloat16)
    y_ref[0] = jnp.where(valid, dot(probs_b, values), 0.0).astype(y_ref.dtype)
    y_ref[1] = jnp.where(valid, dot(score_grad, keys) * SCALING, 0.0).astype(y_ref.dtype)
    key_part = dot(score_grad, q, TN)
    value_part = dot(probs_b, g, TN)

    @pl.when(step == 0)
    def _():
        acc_k[...] = key_part
        acc_v[...] = value_part

    @pl.when(step > 0)
    def _():
        acc_k[...] += key_part
        acc_v[...] += value_part

    @pl.when(step == pl.num_programs(0) - 1)
    def _():
        window = pl.ds(start, WINDOW)
        at = lax.broadcasted_iota(jnp.int32, (WINDOW, 1), 0) + start
        mine = (at >= low) & (at < high)
        dk = (acc_k[...] * SCALING).astype(dk_ref.dtype)
        dv = acc_v[...].astype(dv_ref.dtype)
        if last:
            dk_ref[...] = dk_in[...]
            dv_ref[...] = dv_in[...]
            dk_ref[window, :] = jnp.where(mine, dk, dk_in[window, :])
            dv_ref[window, :] = jnp.where(mine, dv, dv_in[window, :])
        else:
            dk_ref[...] = jnp.zeros_like(dk_ref)
            dv_ref[...] = jnp.zeros_like(dv_ref)
            dk_ref[window, :] = jnp.where(mine, dk, jnp.zeros_like(dk))
            dv_ref[window, :] = jnp.where(mine, dv, jnp.zeros_like(dv))


def attend(scal, x, keys, values, before):
    cap = x.shape[1]
    enc = pl.BlockSpec(keys.shape, lambda i: (0, 0))
    blocks = pl.BlockSpec((2, ROWS, HEAD_DIM), lambda i: (0, i, 0))
    return pl.pallas_call(
        functools.partial(attend_kernel, bool(before)),
        grid=(cap // ROWS,),
        in_specs=[SMEM, blocks, enc, enc] + [enc] * len(before),
        out_specs=[blocks, enc, enc],
        out_shape=[
            jax.ShapeDtypeStruct(x.shape, x.dtype),
            jax.ShapeDtypeStruct(keys.shape, keys.dtype),
            jax.ShapeDtypeStruct(values.shape, values.dtype),
        ],
        scratch_shapes=[pltpu.VMEM((WINDOW, HEAD_DIM), jnp.float32)] * 2,
        compiler_params=pltpu.CompilerParams(vmem_limit_bytes=32 * 2**20),
        cost_estimate=pl.CostEstimate(
            flops=12 * cap * WINDOW * HEAD_DIM, bytes_accessed=4 * 2**20, transcendentals=cap * WINDOW
        ),
    )(scal, x, keys, values, *before)


def local(
    queries,
    encoder_keys,
    encoder_values,
    context_grad,
    encoder_lengths,
    decoder_lengths,
    target_device,
):
    owners = lax.axis_size("dp")
    own = lax.axis_index("dp")
    seq_count = target_device.shape[1]
    query_heads = lax.all_to_all(queries, "mp", split_axis=1, concat_axis=0, tiled=True)
    grad_heads = lax.all_to_all(context_grad, "mp", split_axis=1, concat_axis=0, tiled=True)
    dec_total = query_heads.shape[0]
    dec_cap = dec_total // seq_count
    enc_total = encoder_keys.shape[0]
    shifts = target_device[0]
    col_a = (shifts[0] > shifts[1]).astype(jnp.int32)
    columns = jnp.stack([col_a, 1 - col_a])
    shift = jnp.minimum(shifts[0], shifts[1])
    own_enc = encoder_lengths[own]
    own_dec = decoder_lengths[own]
    dec_offsets = jnp.where(columns == 0, 0, own_dec[0])
    dec_live = own_dec[columns]
    dec_scal = jnp.concatenate([dec_offsets, dec_live])
    low = jnp.where(columns == 0, 0, own_enc[0])
    high = low + own_enc[columns]
    first = jnp.minimum(low // 16 * 16, enc_total - WINDOW)
    query_live = decoder_lengths[(own + shifts[columns]) % owners, columns]
    enc_scal = jnp.stack([first, low, high, query_live], axis=1)
    slot = jax.ShapeDtypeStruct((2, dec_cap, HEAD_DIM), queries.dtype)
    xa, xb = pl.pallas_call(
        pack_kernel,
        in_specs=[SMEM, pl.BlockSpec(), pl.BlockSpec()],
        out_shape=[slot, slot],
        compiler_params=pltpu.CompilerParams(vmem_limit_bytes=32 * 2**20),
    )(dec_scal, query_heads, grad_heads)

    def branch(p):
        half_a = p % Z_LEN == Z_LEN // 2
        half_b = (p + 1) % Z_LEN == Z_LEN // 2

        def run(xa, xb, keys, values, scal):
            xa = shifted(xa, owners, -p, half_a)
            xb = shifted(xb, owners, p + 1, half_b)
            ya, dk, dv = attend(scal[0], xa, keys, values, ())
            ya = shifted(ya, owners, p, -half_a)
            yb, dk, dv = attend(scal[1], xb, keys, values, (dk, dv))
            yb = shifted(yb, owners, -p - 1, -half_b)
            return ya, yb, dk, dv

        return run

    ya, yb, key_grad, value_grad = lax.switch(
        shift - 1,
        [branch(p) for p in range(1, owners // 2)],
        xa, xb, encoder_keys, encoder_values, enc_scal,
    )
    heads = jax.ShapeDtypeStruct((dec_total, HEAD_DIM), queries.dtype)
    context_heads, qgrad_heads = pl.pallas_call(
        merge_kernel,
        in_specs=[SMEM, pl.BlockSpec(), pl.BlockSpec()],
        out_shape=[heads, heads],
        compiler_params=pltpu.CompilerParams(vmem_limit_bytes=32 * 2**20),
    )(dec_scal, ya, yb)
    context, query_grad = (
        lax.all_to_all(context_heads, "mp", split_axis=0, concat_axis=1, tiled=True),
        lax.all_to_all(qgrad_heads, "mp", split_axis=0, concat_axis=1, tiled=True),
    )
    return (context, query_grad, key_grad, value_grad)


def solution(mesh):
    return jax.shard_map(
        local,
        mesh=mesh,
        in_specs=(
            P(("dp", "mp"), None),
            P("dp", "mp"),
            P("dp", "mp"),
            P(("dp", "mp"), None),
            P(),
            P(),
            P(),
        ),
        out_specs=(P(("dp", "mp"), None), P(("dp", "mp"), None), P("dp", "mp"), P("dp", "mp")),
        check_vma=False,
    )
```

```python
import functools

import jax
import jax.numpy as jnp
from jax import lax
from jax.experimental import pallas as pl
from jax.experimental.pallas import tpu as pltpu
from jax.sharding import PartitionSpec as P

HEAD_DIM = 256
SCALING = HEAD_DIM ** (-0.5)
ROWS = 128
RING = 16
SMEM = pl.BlockSpec(memory_space=pltpu.SMEM)
NT = (((1,), (1,)), ((), ()))
TN = (((0,), (0,)), ((), ()))
H, K, DEC_OFF, DEC_LEN, ENC_OFF, ENC_LEN, KEY_LEN, QUERY_LEN = 0, 1, 2, 4, 6, 8, 10, 12
PARAMS = pltpu.CompilerParams(vmem_limit_bytes=32 * 2**20)


def dot(a, b, dims=(((1,), (0,)), ((), ()))):
    return lax.dot_general(a, b, dims, preferred_element_type=jnp.float32)


def passed_along(block, distance):
    owners = lax.axis_size("dp")
    steps = [distance]
    if abs(distance) == RING // 2:
        steps = [distance // 2] * 2
    for step in steps:
        if step:
            block = lax.ppermute(block, "dp", [(i, (i + step) % owners) for i in range(owners)])
    return block


def scalars_kernel(owners, own_ref, enc_ref, dec_ref, target_ref, out_ref):
    own = own_ref[0]
    shift0 = lax.rem(target_ref[0, 0], owners)
    m = jnp.where(lax.rem(shift0, RING) < RING // 2, 0, 1)
    shift = jnp.where(m == 0, shift0, owners - 1 - shift0)
    h = lax.rem(shift, RING)
    k = lax.div(shift, RING)
    out_ref[H] = h
    out_ref[K] = k

    def wrapped(i):
        return lax.rem(i + 2 * owners, owners)

    for n, col in enumerate((m, 1 - m)):
        out_ref[DEC_OFF + n] = jnp.where(col == 0, 0, dec_ref[0, own])
        out_ref[DEC_LEN + n] = dec_ref[col, own]
        up = jnp.where(k == 3, 1 - col, col)
        out_ref[ENC_OFF + n] = jnp.where(up == 0, 0, enc_ref[0, own])
        out_ref[ENC_LEN + n] = enc_ref[up, own]
        sign = 1 - 2 * n
        out_ref[KEY_LEN + n] = enc_ref[col, wrapped(own - sign * RING * k)]
        out_ref[QUERY_LEN + n] = dec_ref[col, wrapped(own + (h if n == 0 else -h - 1))]
    for n in range(QUERY_LEN + 2, out_ref.shape[0]):
        out_ref[n] = 0


def scalars(own, enc, dec, target, owners):
    return pl.pallas_call(
        functools.partial(scalars_kernel, owners),
        in_specs=[SMEM] * 4,
        out_specs=SMEM,
        out_shape=jax.ShapeDtypeStruct((16,), jnp.int32),
    )(own, enc, dec, target)


def one_hot(shape, gap, live):
    slot = lax.broadcasted_iota(jnp.int32, shape, 0)
    packed = lax.broadcasted_iota(jnp.int32, shape, 1)
    return ((packed - slot == gap) & (slot < live)).astype(jnp.float32).astype(jnp.bfloat16)


def pack_kernel(off, count, scal, *refs):
    ins, outs = refs[:count], refs[count:]
    cap = outs[0].shape[1]
    for n, out_ref in enumerate(outs):
        pick = one_hot((cap, ins[0].shape[0]), scal[off + n], scal[off + 2 + n])
        for c, in_ref in enumerate(ins):
            out_ref[c] = dot(pick, in_ref[...]).astype(out_ref.dtype)


def pack(scal, off, arrays, cap):
    slot = jax.ShapeDtypeStruct((len(arrays), cap, HEAD_DIM), arrays[0].dtype)
    return pl.pallas_call(
        functools.partial(pack_kernel, off, len(arrays)),
        in_specs=[SMEM] + [pl.BlockSpec()] * len(arrays),
        out_shape=[slot, slot],
        compiler_params=PARAMS,
    )(scal, *arrays)


def merge_kernel(off, count, scal, a_ref, b_ref, *outs):
    picks = [
        one_hot((a_ref.shape[1], outs[0].shape[0]), scal[off + n], scal[off + 2 + n]) for n in range(2)
    ]
    for c, out_ref in enumerate(outs):
        merged = dot(picks[0], a_ref[c], TN) + dot(picks[1], b_ref[c], TN)
        out_ref[...] = merged.astype(out_ref.dtype)


def merge(scal, off, a, b, total):
    count = a.shape[0]
    packed = jax.ShapeDtypeStruct((total, HEAD_DIM), a.dtype)
    return pl.pallas_call(
        functools.partial(merge_kernel, off, count),
        in_specs=[SMEM, pl.BlockSpec(), pl.BlockSpec()],
        out_shape=[packed] * count,
        compiler_params=PARAMS,
    )(scal, a, b)


def softmax(q, keys, live):
    scores = dot(q, keys, NT) * SCALING
    col = lax.broadcasted_iota(jnp.int32, (1, scores.shape[1]), 1)
    scores = jnp.where(col < live, scores, -1e30)
    raised = jnp.exp(scores - jnp.max(scores, axis=1, keepdims=True))
    return raised * (1.0 / jnp.sum(raised, axis=1, keepdims=True))


def context_kernel(n, scal, q_ref, kv_ref, ctx_ref):
    rows = q_ref.shape[1]
    valid = lax.broadcasted_iota(jnp.int32, (rows, 1), 0) + pl.program_id(0) * rows < scal[QUERY_LEN + n]
    probs = softmax(q_ref[0], kv_ref[0], scal[KEY_LEN + n]).astype(jnp.bfloat16)
    ctx_ref[0] = jnp.where(valid, dot(probs, kv_ref[1]), 0.0).astype(ctx_ref.dtype)


def grads_kernel(n, scal, q_ref, g_ref, kv_ref, dq_ref, dkv_ref, acc_ref):
    step = pl.program_id(0)
    rows = q_ref.shape[1]
    valid = lax.broadcasted_iota(jnp.int32, (rows, 1), 0) + step * rows < scal[QUERY_LEN + n]
    q, g, keys = q_ref[0], g_ref[0], kv_ref[0]
    probs = softmax(q, keys, scal[KEY_LEN + n])
    prob_grad = dot(g, kv_ref[1], NT)
    row_dot = jnp.sum(probs * prob_grad, axis=1, keepdims=True)
    score_grad = (probs * (prob_grad - row_dot)).astype(jnp.bfloat16)
    dq_ref[0] = jnp.where(valid, dot(score_grad, keys) * SCALING, 0.0).astype(dq_ref.dtype)

    @pl.when(step == 0)
    def _():
        acc_ref[...] = jnp.zeros_like(acc_ref)

    acc_ref[0] += dot(score_grad, q, TN)
    acc_ref[1] += dot(probs.astype(jnp.bfloat16), g, TN)

    @pl.when(step == pl.num_programs(0) - 1)
    def _():
        dkv_ref[0] = (acc_ref[0] * SCALING).astype(dkv_ref.dtype)
        dkv_ref[1] = acc_ref[1].astype(dkv_ref.dtype)


def whole(shape):
    return pl.BlockSpec(shape, lambda i: (0,) * len(shape))


BLOCKS = pl.BlockSpec((1, ROWS, HEAD_DIM), lambda i: (0, i, 0))


def context_of(n, scal, q, kv):
    cap, keys = q.shape[1], kv.shape[1]
    return pl.pallas_call(
        functools.partial(context_kernel, n),
        grid=(cap // ROWS,),
        in_specs=[SMEM, BLOCKS, whole(kv.shape)],
        out_specs=BLOCKS,
        out_shape=jax.ShapeDtypeStruct(q.shape, q.dtype),
        compiler_params=PARAMS,
        cost_estimate=pl.CostEstimate(
            flops=4 * cap * keys * HEAD_DIM, bytes_accessed=2 * 2**20, transcendentals=cap * keys
        ),
    )(scal, q, kv)


def grads_of(n, scal, q, g, kv):
    cap, keys = q.shape[1], kv.shape[1]
    return pl.pallas_call(
        functools.partial(grads_kernel, n),
        grid=(cap // ROWS,),
        in_specs=[SMEM, BLOCKS, BLOCKS, whole(kv.shape)],
        out_specs=[BLOCKS, whole(kv.shape)],
        out_shape=[jax.ShapeDtypeStruct(q.shape, q.dtype), jax.ShapeDtypeStruct(kv.shape, kv.dtype)],
        scratch_shapes=[pltpu.VMEM(kv.shape, jnp.float32)],
        compiler_params=PARAMS,
        cost_estimate=pl.CostEstimate(
            flops=10 * cap * keys * HEAD_DIM, bytes_accessed=3 * 2**20, transcendentals=cap * keys
        ),
    )(scal, q, g, kv)


def chosen(k, options):
    out = options[0]
    for n in range(1, len(options)):
        out = jnp.where(k == n, options[n], out)
    return out


def to_heads(rows):
    return lax.all_to_all(rows, "mp", split_axis=1, concat_axis=0, tiled=True)


def to_tokens(heads):
    return lax.all_to_all(heads, "mp", split_axis=0, concat_axis=1, tiled=True)


def local(
    queries,
    encoder_keys,
    encoder_values,
    context_grad,
    encoder_lengths,
    decoder_lengths,
    target_device,
):
    owners = lax.axis_size("dp")
    own = lax.axis_index("dp").astype(jnp.int32).reshape(1)
    seq_count = target_device.shape[1]
    dec_total = queries.shape[0] * lax.axis_size("mp")
    dec_cap = dec_total // seq_count
    enc_total = encoder_keys.shape[0]
    enc_cap = enc_total // seq_count
    scal = scalars(own, encoder_lengths.T, decoder_lengths.T, target_device.T, owners)
    k = scal[K]
    up0, down0 = pack(scal, ENC_OFF, [encoder_keys, encoder_values], enc_cap)
    up1 = passed_along(up0, RING)
    down1 = passed_along(down0, -RING)
    qm, qn = pack(scal, DEC_OFF, [to_heads(queries)], dec_cap)

    def branch(h):
        def run(scal, k, qm, qn, context_grad, up0, down0, up1, down1):
            qm = passed_along(qm, -h)
            qn = passed_along(qn, h + 1)
            gm, gn = pack(scal, DEC_OFF, [to_heads(context_grad)], dec_cap)
            gm = passed_along(gm, -h)
            gn = passed_along(gn, h + 1)
            up2 = passed_along(up1, RING)
            down2 = passed_along(down1, -RING)
            kv_m = chosen(k, [up0, up1, up2, down1])
            kv_n = chosen(k, [down0, down1, down2, up1])
            cm = passed_along(context_of(0, scal, qm, kv_m), h)
            cn = passed_along(context_of(1, scal, qn, kv_n), -h - 1)
            dqm, dkv_m = grads_of(0, scal, qm, gm, kv_m)
            dqm = passed_along(dqm, h)
            dqn, dkv_n = grads_of(1, scal, qn, gn, kv_n)
            dqn = passed_along(dqn, -h - 1)
            down = jnp.where(k == 3, dkv_n, dkv_m)
            up = jnp.where(k == 3, dkv_m, dkv_n)
            down_back = passed_along(down, -RING)
            up_back = passed_along(up, RING)
            (ctx,) = merge(scal, DEC_OFF, cm, cn, dec_total)
            context = to_tokens(ctx)
            return context, dqm, dqn, down, up, down_back, up_back

        return run

    context, dqm, dqn, down0, up0, down1, up1 = lax.switch(
        scal[H],
        [branch(h) for h in range(RING // 2)],
        scal, k, qm, qn, context_grad, up0, down0, up1, down1,
    )
    down2 = passed_along(down1, -RING)
    up2 = passed_along(up1, RING)
    (dq,) = merge(scal, DEC_OFF, dqm, dqn, dec_total)
    query_grad = to_tokens(dq)
    first = chosen(k, [down0, down1, down2, down1])
    second = chosen(k, [up0, up1, up2, up1])
    key_grad, value_grad = merge(scal, ENC_OFF, first, second, enc_total)
    return (context, query_grad, key_grad, value_grad)


def solution(mesh):
    return jax.shard_map(
        local,
        mesh=mesh,
        in_specs=(
            P(("dp", "mp"), None),
            P("dp", "mp"),
            P("dp", "mp"),
            P(("dp", "mp"), None),
            P(),
            P(),
            P(),
        ),
        out_specs=(P(("dp", "mp"), None), P(("dp", "mp"), None), P("dp", "mp"), P("dp", "mp")),
        check_vma=False,
    )
```

```python
import functools

import jax
import jax.numpy as jnp
from jax import lax
from jax.experimental import pallas as pl
from jax.experimental.pallas import tpu as pltpu
from jax.sharding import PartitionSpec as P

HEAD_DIM = 256
SCALING = HEAD_DIM ** (-0.5)
ROWS = 128
RING = 16
KEY_HOPS = 2
SMEM = pl.BlockSpec(memory_space=pltpu.SMEM)
NT = (((1,), (1,)), ((), ()))
TN = (((0,), (0,)), ((), ()))
H, K, DEC_OFF, DEC_LEN, ENC_OFF, ENC_LEN, KEY_LEN, QUERY_LEN = 0, 1, 2, 4, 6, 8, 10, 12
PARAMS = pltpu.CompilerParams(vmem_limit_bytes=32 * 2**20)


def dot(a, b, dims=(((1,), (0,)), ((), ()))):
    return lax.dot_general(a, b, dims, preferred_element_type=jnp.float32)


def passed_along(block, distance):
    owners = lax.axis_size("dp")
    if distance % owners == 0:
        return block
    return lax.ppermute(block, "dp", [(i, (i + distance) % owners) for i in range(owners)])


def one_hot(shape, gap, live):
    slot = lax.broadcasted_iota(jnp.int32, shape, 0)
    packed = lax.broadcasted_iota(jnp.int32, shape, 1)
    return ((packed - slot == gap) & (slot < live)).astype(jnp.float32).astype(jnp.bfloat16)


def prepare_kernel(
    owners, own_ref, enc_ref, dec_ref, target_ref, k_ref, v_ref, q_ref, g_ref, out_ref, kvm_ref, kvn_ref, parts_ref
):
    for j in range(parts_ref.shape[0]):
        for c, in_ref in enumerate((q_ref, g_ref)):
            parts_ref[j, c] = in_ref[:, j * HEAD_DIM : (j + 1) * HEAD_DIM]
    own = own_ref[0]
    shift0 = lax.rem(target_ref[0, 0], owners)
    m = jnp.where(lax.rem(shift0, RING) < RING // 2, 0, 1)
    shift = jnp.where(m == 0, shift0, owners - 1 - shift0)
    h = lax.rem(shift, RING)
    k = lax.div(shift, RING)
    out_ref[H] = h
    out_ref[K] = k

    def wrapped(i):
        return lax.rem(i + 2 * owners, owners)

    for n, kv_ref in enumerate((kvm_ref, kvn_ref)):
        col = m if n == 0 else 1 - m
        sign = 1 - 2 * n
        hops = jnp.minimum(h + n, KEY_HOPS)
        off = jnp.where(col == 0, 0, enc_ref[0, own])
        live = enc_ref[col, own]
        out_ref[DEC_OFF + n] = jnp.where(col == 0, 0, dec_ref[0, own])
        out_ref[DEC_LEN + n] = dec_ref[col, own]
        out_ref[ENC_OFF + n] = off
        out_ref[ENC_LEN + n] = live
        out_ref[KEY_LEN + n] = enc_ref[col, wrapped(own - sign * (RING * k + hops))]
        out_ref[QUERY_LEN + n] = dec_ref[col, wrapped(own + sign * (h + n - hops))]
        pick = one_hot((kv_ref.shape[1], k_ref.shape[0]), off, live)
        kv_ref[0] = dot(pick, k_ref[...]).astype(kv_ref.dtype)
        kv_ref[1] = dot(pick, v_ref[...]).astype(kv_ref.dtype)
    for n in range(QUERY_LEN + 2, out_ref.shape[0]):
        out_ref[n] = 0


def prepare(own, enc, dec, target, keys, values, queries, grads, owners, cap):
    slot = jax.ShapeDtypeStruct((2, cap, HEAD_DIM), keys.dtype)
    rows, width = queries.shape
    parts = jax.ShapeDtypeStruct((width // HEAD_DIM, 2, rows, HEAD_DIM), queries.dtype)
    return pl.pallas_call(
        functools.partial(prepare_kernel, owners),
        in_specs=[SMEM] * 4 + [pl.BlockSpec()] * 4,
        out_specs=[SMEM] + [pl.BlockSpec()] * 3,
        out_shape=[jax.ShapeDtypeStruct((16,), jnp.int32), slot, slot, parts],
        compiler_params=PARAMS,
    )(own, enc, dec, target, keys, values, queries, grads)


def pack_kernel(scal, in_ref, *outs):
    total = in_ref.shape[0] * in_ref.shape[2]
    for n, out_ref in enumerate(outs):
        pick = one_hot((out_ref.shape[1], total), scal[DEC_OFF + n], scal[DEC_LEN + n])
        for c in range(in_ref.shape[1]):
            rows = in_ref[:, c].reshape(total, HEAD_DIM)
            out_ref[c] = dot(pick, rows).astype(out_ref.dtype)


def pack(scal, heads, cap):
    slot = jax.ShapeDtypeStruct((heads.shape[1], cap, HEAD_DIM), heads.dtype)
    return pl.pallas_call(
        pack_kernel,
        in_specs=[SMEM, pl.BlockSpec()],
        out_shape=[slot, slot],
        compiler_params=PARAMS,
    )(scal, heads)


def merge_kernel(off, total, scal, a_ref, b_ref, *outs):
    picks = [one_hot((a_ref.shape[1], total), scal[off + n], scal[off + 2 + n]) for n in range(2)]
    for c in range(a_ref.shape[0]):
        merged = (dot(picks[0], a_ref[c], TN) + dot(picks[1], b_ref[c], TN)).astype(outs[0].dtype)
        if len(outs) == 1:
            outs[0][:, c] = merged.reshape(outs[0].shape[0], outs[0].shape[2], HEAD_DIM)
        else:
            outs[c][...] = merged


def merge(scal, off, a, b, total, parts):
    if parts > 1:
        packed = [jax.ShapeDtypeStruct((parts, a.shape[0], total // parts, HEAD_DIM), a.dtype)]
    else:
        packed = [jax.ShapeDtypeStruct((total, HEAD_DIM), a.dtype)] * a.shape[0]
    return pl.pallas_call(
        functools.partial(merge_kernel, off, total),
        in_specs=[SMEM, pl.BlockSpec(), pl.BlockSpec()],
        out_shape=packed,
        compiler_params=PARAMS,
    )(scal, a, b)


def attend_kernel(n, scal, x_ref, kv_ref, y_ref, dkv_ref, acc_ref):
    step = pl.program_id(0)
    rows = x_ref.shape[1]
    valid = lax.broadcasted_iota(jnp.int32, (rows, 1), 0) + step * rows < scal[QUERY_LEN + n]
    q, g, keys, values = x_ref[0], x_ref[1], kv_ref[0], kv_ref[1]
    scores = dot(q, keys, NT) * SCALING
    col = lax.broadcasted_iota(jnp.int32, (1, scores.shape[1]), 1)
    scores = jnp.where(col < scal[KEY_LEN + n], scores, -1e30)
    raised = jnp.exp(scores - jnp.max(scores, axis=1, keepdims=True))
    probs = raised * (1.0 / jnp.sum(raised, axis=1, keepdims=True))
    probs_b = probs.astype(jnp.bfloat16)
    prob_grad = dot(g, values, NT)
    row_dot = jnp.sum(probs * prob_grad, axis=1, keepdims=True)
    score_grad = (probs * (prob_grad - row_dot)).astype(jnp.bfloat16)
    y_ref[0] = jnp.where(valid, dot(probs_b, values), 0.0).astype(y_ref.dtype)
    y_ref[1] = jnp.where(valid, dot(score_grad, keys) * SCALING, 0.0).astype(y_ref.dtype)

    @pl.when(step == 0)
    def _():
        acc_ref[...] = jnp.zeros_like(acc_ref)

    acc_ref[0] += dot(score_grad, q, TN)
    acc_ref[1] += dot(probs_b, g, TN)

    @pl.when(step == pl.num_programs(0) - 1)
    def _():
        dkv_ref[0] = (acc_ref[0] * SCALING).astype(dkv_ref.dtype)
        dkv_ref[1] = acc_ref[1].astype(dkv_ref.dtype)


def attend(n, scal, x, kv):
    cap, keys = x.shape[1], kv.shape[1]
    blocks = pl.BlockSpec((2, ROWS, HEAD_DIM), lambda i: (0, i, 0))
    whole = pl.BlockSpec(kv.shape, lambda i: (0, 0, 0))
    return pl.pallas_call(
        functools.partial(attend_kernel, n),
        grid=(cap // ROWS,),
        in_specs=[SMEM, blocks, whole],
        out_specs=[blocks, whole],
        out_shape=[jax.ShapeDtypeStruct(x.shape, x.dtype), jax.ShapeDtypeStruct(kv.shape, kv.dtype)],
        scratch_shapes=[pltpu.VMEM(kv.shape, jnp.float32)],
        compiler_params=PARAMS,
        cost_estimate=pl.CostEstimate(
            flops=12 * cap * keys * HEAD_DIM, bytes_accessed=3 * 2**20, transcendentals=cap * keys
        ),
    )(scal, x, kv)


def exchanged(parts):
    return lax.all_to_all(parts, "mp", split_axis=0, concat_axis=0, tiled=True)


def to_tokens(heads):
    size, count, rows, _ = heads.shape
    parts = exchanged(heads)
    return [parts[:, n].transpose(1, 0, 2).reshape(rows, size * HEAD_DIM) for n in range(count)]


def local(
    queries,
    encoder_keys,
    encoder_values,
    context_grad,
    encoder_lengths,
    decoder_lengths,
    target_device,
):
    owners = lax.axis_size("dp")
    own = lax.axis_index("dp").astype(jnp.int32).reshape(1)
    seq_count = target_device.shape[1]
    dec_total = queries.shape[0] * lax.axis_size("mp")
    dec_cap = dec_total // seq_count
    enc_total = encoder_keys.shape[0]
    enc_cap = enc_total // seq_count
    scal, kvm, kvn, parts = prepare(
        own, encoder_lengths.T, decoder_lengths.T, target_device.T,
        encoder_keys, encoder_values, queries, context_grad, owners, enc_cap,
    )
    h, k = scal[H], scal[K]
    ways = [
        (RING * i + min(j, KEY_HOPS), RING * i + min(j + 1, KEY_HOPS))
        for i in range(owners // RING)
        for j in range(KEY_HOPS + 1)
    ]
    way = k * (KEY_HOPS + 1) + jnp.minimum(h, KEY_HOPS)

    def out_along(m, n):
        def run(kvm, kvn, parts):
            return passed_along(kvm, m), passed_along(kvn, -n), exchanged(parts)

        return run

    kvm, kvn, heads = lax.switch(way, [out_along(*w) for w in ways], kvm, kvn, parts)
    xm, xn = pack(scal, heads, dec_cap)

    def around(m, n):
        def run(scal, xm, xn, kvm, kvn):
            xm = passed_along(xm, -m)
            xn = passed_along(xn, n)
            ym, kvm = attend(0, scal, xm, kvm)
            ym = passed_along(ym, m)
            yn, kvn = attend(1, scal, xn, kvn)
            yn = passed_along(yn, -n)
            return ym, yn, kvm, kvn

        return run

    ym, yn, kvm, kvn = lax.switch(
        jnp.maximum(h, KEY_HOPS - 1) - (KEY_HOPS - 1),
        [around(max(j - KEY_HOPS, 0), j + 1 - KEY_HOPS) for j in range(KEY_HOPS - 1, RING // 2)],
        scal, xm, xn, kvm, kvn,
    )
    (heads,) = merge(scal, DEC_OFF, ym, yn, dec_total, lax.axis_size("mp"))

    def back_along(m, n):
        def run(kvm, kvn, heads):
            return passed_along(kvm, -m), passed_along(kvn, n), *to_tokens(heads)

        return run

    kvm, kvn, context, query_grad = lax.switch(way, [back_along(*w) for w in ways], kvm, kvn, heads)
    key_grad, value_grad = merge(scal, ENC_OFF, kvm, kvn, enc_total, 1)
    return (context, query_grad, key_grad, value_grad)


def solution(mesh):
    return jax.shard_map(
        local,
        mesh=mesh,
        in_specs=(
            P(("dp", "mp"), None),
            P("dp", "mp"),
            P("dp", "mp"),
            P(("dp", "mp"), None),
            P(),
            P(),
            P(),
        ),
        out_specs=(P(("dp", "mp"), None), P(("dp", "mp"), None), P("dp", "mp"), P("dp", "mp")),
        check_vma=False,
    )
```

```python
import functools

import jax
import jax.numpy as jnp
from jax import lax
from jax.experimental import pallas as pl
from jax.experimental.pallas import tpu as pltpu
from jax.sharding import PartitionSpec as P

HEAD_DIM = 256
SCALING = HEAD_DIM ** (-0.5)
ROWS = 256
RING = 16
KEY_HOPS = 2
SMEM = pl.BlockSpec(memory_space=pltpu.SMEM)
NT = (((1,), (1,)), ((), ()))
TN = (((0,), (0,)), ((), ()))
H, K, COL, DEC_LEN, ENC_LEN, KEY_LEN, QUERY_LEN = 0, 1, 2, 4, 6, 8, 10
PARAMS = pltpu.CompilerParams(vmem_limit_bytes=32 * 2**20)


def dot(a, b, dims=(((1,), (0,)), ((), ()))):
    return lax.dot_general(a, b, dims, preferred_element_type=jnp.float32)


def passed_along(block, distance):
    owners = lax.axis_size("dp")
    if distance % owners == 0:
        return block
    return lax.ppermute(block, "dp", [(i, (i + distance) % owners) for i in range(owners)])


def one_hot(shape, gap, live):
    row = lax.broadcasted_iota(jnp.int32, shape, 0)
    col = lax.broadcasted_iota(jnp.int32, shape, 1)
    return ((col - row == gap) & (col < live)).astype(jnp.float32).astype(jnp.bfloat16)


def unpacked(m, len0, len1, arrays, m_ref, n_ref):
    total, cap = arrays[0].shape[0], m_ref.shape[1]
    pick = one_hot((cap, total), len0, len0 + len1)
    live = lax.broadcasted_iota(jnp.int32, (cap, 1), 0) < len0
    for c, rows in enumerate(arrays):
        first = jnp.where(live, rows[:cap], jnp.zeros_like(rows[:cap]))
        second = dot(pick, rows).astype(rows.dtype)
        m_ref[c] = jnp.where(m == 0, first, second)
        n_ref[c] = jnp.where(m == 0, second, first)


def packed(m, len0, len1, a, b, total):
    cap = a.shape[0]
    first = jnp.where(m == 0, a, b)
    second = jnp.where(m == 0, b, a)
    live = lax.broadcasted_iota(jnp.int32, (cap, 1), 0) < len0
    first = jnp.where(live, first, jnp.zeros_like(first)).astype(jnp.float32)
    moved = dot(one_hot((total, cap), -len0, len1), second)
    return jnp.concatenate([moved[:cap] + first, moved[cap:]], axis=0).astype(a.dtype)


def prepare_kernel(owners, own_ref, enc_ref, dec_ref, target_ref, k_ref, v_ref, out_ref, kvm_ref, kvn_ref):
    own = own_ref[0]
    shift0 = lax.rem(target_ref[0, 0], owners)
    m = jnp.where(lax.rem(shift0, RING) < RING // 2, 0, 1)
    shift = jnp.where(m == 0, shift0, owners - 1 - shift0)
    h = lax.rem(shift, RING)
    k = lax.div(shift, RING)
    out_ref[H] = h
    out_ref[K] = k
    out_ref[COL] = m
    out_ref[COL + 1] = 0

    def wrapped(i):
        return lax.rem(i + 2 * owners, owners)

    for n in range(2):
        col = m if n == 0 else 1 - m
        sign = 1 - 2 * n
        hops = jnp.minimum(h + n, KEY_HOPS)
        out_ref[DEC_LEN + n] = dec_ref[n, own]
        out_ref[ENC_LEN + n] = enc_ref[n, own]
        out_ref[KEY_LEN + n] = enc_ref[col, wrapped(own - sign * (RING * k + hops))]
        out_ref[QUERY_LEN + n] = dec_ref[col, wrapped(own + sign * (h + n - hops))]
    for n in range(QUERY_LEN + 2, out_ref.shape[0]):
        out_ref[n] = 0
    unpacked(m, enc_ref[0, own], enc_ref[1, own], (k_ref[...], v_ref[...]), kvm_ref, kvn_ref)


def prepare(own, enc, dec, target, keys, values, owners, cap):
    slot = jax.ShapeDtypeStruct((2, cap, HEAD_DIM), keys.dtype)
    return pl.pallas_call(
        functools.partial(prepare_kernel, owners),
        in_specs=[SMEM] * 4 + [pl.BlockSpec()] * 2,
        out_specs=[SMEM] + [pl.BlockSpec()] * 2,
        out_shape=[jax.ShapeDtypeStruct((16,), jnp.int32), slot, slot],
        compiler_params=PARAMS,
    )(own, enc, dec, target, keys, values)


def split_kernel(q_ref, g_ref, parts_ref):
    for j in range(parts_ref.shape[0]):
        for c, in_ref in enumerate((q_ref, g_ref)):
            parts_ref[j, c] = in_ref[:, j * HEAD_DIM : (j + 1) * HEAD_DIM]


def split(queries, grads):
    rows, width = queries.shape
    return pl.pallas_call(
        split_kernel,
        out_shape=jax.ShapeDtypeStruct((width // HEAD_DIM, 2, rows, HEAD_DIM), queries.dtype),
        compiler_params=PARAMS,
    )(queries, grads)


def join_kernel(parts_ref, *outs):
    for j in range(parts_ref.shape[0]):
        for c, out_ref in enumerate(outs):
            out_ref[:, j * HEAD_DIM : (j + 1) * HEAD_DIM] = parts_ref[j, c]


def join(parts):
    heads, count, rows, _ = parts.shape
    return pl.pallas_call(
        join_kernel,
        out_shape=[jax.ShapeDtypeStruct((rows, heads * HEAD_DIM), parts.dtype)] * count,
        compiler_params=PARAMS,
    )(parts)


def pack_kernel(scal, in_ref, xm_ref, xn_ref):
    arrays = [in_ref[:, c].reshape(-1, HEAD_DIM) for c in range(in_ref.shape[1])]
    unpacked(scal[COL], scal[DEC_LEN], scal[DEC_LEN + 1], arrays, xm_ref, xn_ref)


def pack(scal, parts, cap):
    slot = jax.ShapeDtypeStruct((parts.shape[1], cap, HEAD_DIM), parts.dtype)
    return pl.pallas_call(
        pack_kernel,
        in_specs=[SMEM, pl.BlockSpec()],
        out_shape=[slot, slot],
        compiler_params=PARAMS,
    )(scal, parts)


def merge_kernel(length, total, scal, a_ref, b_ref, *outs):
    for c in range(a_ref.shape[0]):
        rows = packed(scal[COL], scal[length], scal[length + 1], a_ref[c], b_ref[c], total)
        if len(outs) == 1:
            outs[0][:, c] = rows.reshape(outs[0].shape[0], outs[0].shape[2], HEAD_DIM)
        else:
            outs[c][...] = rows


def merge(scal, length, a, b, total, parts):
    if parts > 1:
        out = [jax.ShapeDtypeStruct((parts, a.shape[0], total // parts, HEAD_DIM), a.dtype)]
    else:
        out = [jax.ShapeDtypeStruct((total, HEAD_DIM), a.dtype)] * a.shape[0]
    return pl.pallas_call(
        functools.partial(merge_kernel, length, total),
        in_specs=[SMEM, pl.BlockSpec(), pl.BlockSpec()],
        out_shape=out,
        compiler_params=PARAMS,
    )(scal, a, b)


def attend_kernel(n, scal, x_ref, kv_ref, y_ref, dkv_ref, acc_ref):
    step = pl.program_id(0)
    rows = x_ref.shape[1]
    valid = lax.broadcasted_iota(jnp.int32, (rows, 1), 0) + step * rows < scal[QUERY_LEN + n]
    q, g, keys, values = x_ref[0], x_ref[1], kv_ref[0], kv_ref[1]
    scores = dot(q, keys, NT) * SCALING
    col = lax.broadcasted_iota(jnp.int32, (1, scores.shape[1]), 1)
    scores = jnp.where(col < scal[KEY_LEN + n], scores, -1e30)
    raised = jnp.exp(scores - jnp.max(scores, axis=1, keepdims=True))
    probs = raised * (1.0 / jnp.sum(raised, axis=1, keepdims=True))
    probs_b = probs.astype(jnp.bfloat16)
    prob_grad = dot(g, values, NT)
    row_dot = jnp.sum(probs * prob_grad, axis=1, keepdims=True)
    score_grad = (probs * (prob_grad - row_dot)).astype(jnp.bfloat16)
    y_ref[0] = jnp.where(valid, dot(probs_b, values), 0.0).astype(y_ref.dtype)
    y_ref[1] = jnp.where(valid, dot(score_grad, keys) * SCALING, 0.0).astype(y_ref.dtype)

    @pl.when(step == 0)
    def _():
        acc_ref[...] = jnp.zeros_like(acc_ref)

    acc_ref[0] += dot(score_grad, q, TN)
    acc_ref[1] += dot(probs_b, g, TN)

    @pl.when(step == pl.num_programs(0) - 1)
    def _():
        dkv_ref[0] = (acc_ref[0] * SCALING).astype(dkv_ref.dtype)
        dkv_ref[1] = acc_ref[1].astype(dkv_ref.dtype)


def attend(n, scal, x, kv):
    cap, keys = x.shape[1], kv.shape[1]
    blocks = pl.BlockSpec((2, ROWS, HEAD_DIM), lambda i: (0, i, 0))
    whole = pl.BlockSpec(kv.shape, lambda i: (0, 0, 0))
    return pl.pallas_call(
        functools.partial(attend_kernel, n),
        grid=(cap // ROWS,),
        in_specs=[SMEM, blocks, whole],
        out_specs=[blocks, whole],
        out_shape=[jax.ShapeDtypeStruct(x.shape, x.dtype), jax.ShapeDtypeStruct(kv.shape, kv.dtype)],
        scratch_shapes=[pltpu.VMEM(kv.shape, jnp.float32)],
        compiler_params=PARAMS,
        cost_estimate=pl.CostEstimate(
            flops=12 * cap * keys * HEAD_DIM, bytes_accessed=3 * 2**20, transcendentals=cap * keys
        ),
    )(scal, x, kv)


def exchanged(parts):
    return lax.all_to_all(parts, "mp", split_axis=0, concat_axis=0, tiled=True)


def local(
    queries,
    encoder_keys,
    encoder_values,
    context_grad,
    encoder_lengths,
    decoder_lengths,
    target_device,
):
    owners = lax.axis_size("dp")
    own = lax.axis_index("dp").astype(jnp.int32).reshape(1)
    seq_count = target_device.shape[1]
    dec_total = queries.shape[0] * lax.axis_size("mp")
    dec_cap = dec_total // seq_count
    enc_total = encoder_keys.shape[0]
    enc_cap = enc_total // seq_count
    scal, kvm, kvn = prepare(
        own, encoder_lengths.T, decoder_lengths.T, target_device.T, encoder_keys, encoder_values, owners, enc_cap
    )
    h, k = scal[H], scal[K]
    ways = [
        (RING * i + min(j, KEY_HOPS), RING * i + min(j + 1, KEY_HOPS))
        for i in range(owners // RING)
        for j in range(KEY_HOPS + 1)
    ]
    way = k * (KEY_HOPS + 1) + jnp.minimum(h, KEY_HOPS)

    def out_along(m, n):
        def run(scal, kvm, kvn, queries, context_grad):
            xm, xn = pack(scal, exchanged(split(queries, context_grad)), dec_cap)
            return passed_along(kvm, m), passed_along(kvn, -n), xm, xn

        return run

    kvm, kvn, xm, xn = lax.switch(
        way, [out_along(*w) for w in ways], scal, kvm, kvn, queries, context_grad
    )

    def around(m, n):
        def run(scal, xm, xn, kvm, kvn):
            xm = passed_along(xm, -m)
            xn = passed_along(xn, n)
            ym, kvm = attend(0, scal, xm, kvm)
            ym = passed_along(ym, m)
            yn, kvn = attend(1, scal, xn, kvn)
            yn = passed_along(yn, -n)
            return ym, yn, kvm, kvn

        return run

    ym, yn, kvm, kvn = lax.switch(
        jnp.maximum(h, KEY_HOPS - 1) - (KEY_HOPS - 1),
        [around(max(j - KEY_HOPS, 0), j + 1 - KEY_HOPS) for j in range(KEY_HOPS - 1, RING // 2)],
        scal, xm, xn, kvm, kvn,
    )

    def back_along(m, n):
        def run(scal, kvm, kvn, ym, yn):
            (parts,) = merge(scal, DEC_LEN, ym, yn, dec_total, lax.axis_size("mp"))
            return passed_along(kvm, -m), passed_along(kvn, n), *join(exchanged(parts))

        return run

    kvm, kvn, context, query_grad = lax.switch(way, [back_along(*w) for w in ways], scal, kvm, kvn, ym, yn)
    key_grad, value_grad = merge(scal, ENC_LEN, kvm, kvn, enc_total, 1)
    return (context, query_grad, key_grad, value_grad)


def solution(mesh):
    return jax.shard_map(
        local,
        mesh=mesh,
        in_specs=(
            P(("dp", "mp"), None),
            P("dp", "mp"),
            P("dp", "mp"),
            P(("dp", "mp"), None),
            P(),
            P(),
            P(),
        ),
        out_specs=(P(("dp", "mp"), None), P(("dp", "mp"), None), P("dp", "mp"), P("dp", "mp")),
        check_vma=False,
    )
```

```python
import functools

import jax
import jax.numpy as jnp
from jax import lax
from jax.experimental import pallas as pl
from jax.experimental.pallas import tpu as pltpu
from jax.sharding import PartitionSpec as P

HEAD_DIM = 256
SCALING = HEAD_DIM ** (-0.5)
ROWS = 256
RING = 16
KEY_HOPS = 2
SMEM = pl.BlockSpec(memory_space=pltpu.SMEM)
NT = (((1,), (1,)), ((), ()))
TN = (((0,), (0,)), ((), ()))
WAY, AROUND, COL, DEC_LEN, ENC_LEN, KEY_LEN, QUERY_LEN = 0, 1, 2, 4, 6, 8, 10
PARAMS = pltpu.CompilerParams(vmem_limit_bytes=32 * 2**20)


def dot(a, b, dims=(((1,), (0,)), ((), ()))):
    return lax.dot_general(a, b, dims, preferred_element_type=jnp.float32)


def passed_along(block, distance):
    owners = lax.axis_size("dp")
    if distance % owners == 0:
        return block
    return lax.ppermute(block, "dp", [(i, (i + distance) % owners) for i in range(owners)])


def one_hot(shape, gap, live):
    row = lax.broadcasted_iota(jnp.int32, shape, 0)
    col = lax.broadcasted_iota(jnp.int32, shape, 1)
    return ((col - row == gap) & (col < live)).astype(jnp.float32).astype(jnp.bfloat16)


def unpacked(m, len0, len1, arrays, m_ref, n_ref):
    total, cap = arrays[0].shape[0], m_ref.shape[1]
    pick = one_hot((cap, total), len0, len0 + len1)
    live = lax.broadcasted_iota(jnp.int32, (cap, 1), 0) < len0
    for c, rows in enumerate(arrays):
        first = jnp.where(live, rows[:cap], jnp.zeros_like(rows[:cap]))
        second = dot(pick, rows).astype(rows.dtype)
        m_ref[c] = jnp.where(m == 0, first, second)
        n_ref[c] = jnp.where(m == 0, second, first)


def packed(m, len0, len1, a, b, total):
    cap = a.shape[0]
    first = jnp.where(m == 0, a, b)
    second = jnp.where(m == 0, b, a)
    live = lax.broadcasted_iota(jnp.int32, (cap, 1), 0) < len0
    first = jnp.where(live, first, jnp.zeros_like(first)).astype(jnp.float32)
    moved = dot(one_hot((total, cap), -len0, len1), second)
    return jnp.concatenate([moved[:cap] + first, moved[cap:]], axis=0).astype(a.dtype)


def prepare_kernel(owners, own_ref, enc_ref, dec_ref, target_ref, k_ref, v_ref, out_ref, kvm_ref, kvn_ref):
    own = own_ref[0]
    shift0 = lax.rem(target_ref[0, 0], owners)
    m = jnp.where(lax.rem(shift0, RING) < RING // 2, 0, 1)
    shift = jnp.where(m == 0, shift0, owners - 1 - shift0)
    h = lax.rem(shift, RING)
    k = lax.div(shift, RING)
    out_ref[WAY] = k * (KEY_HOPS + 1) + jnp.minimum(h, KEY_HOPS)
    out_ref[AROUND] = jnp.maximum(h, KEY_HOPS - 1) - (KEY_HOPS - 1)
    out_ref[COL] = m
    out_ref[COL + 1] = 0

    def wrapped(i):
        return lax.rem(i + 2 * owners, owners)

    for n in range(2):
        col = m if n == 0 else 1 - m
        sign = 1 - 2 * n
        hops = jnp.minimum(h + n, KEY_HOPS)
        out_ref[DEC_LEN + n] = dec_ref[n, own]
        out_ref[ENC_LEN + n] = enc_ref[n, own]
        out_ref[KEY_LEN + n] = enc_ref[col, wrapped(own - sign * (RING * k + hops))]
        out_ref[QUERY_LEN + n] = dec_ref[col, wrapped(own + sign * (h + n - hops))]
    for n in range(QUERY_LEN + 2, out_ref.shape[0]):
        out_ref[n] = 0
    unpacked(m, enc_ref[0, own], enc_ref[1, own], (k_ref[...], v_ref[...]), kvm_ref, kvn_ref)


def prepare(own, enc, dec, target, keys, values, owners, cap):
    slot = jax.ShapeDtypeStruct((2, cap, HEAD_DIM), keys.dtype)
    return pl.pallas_call(
        functools.partial(prepare_kernel, owners),
        in_specs=[SMEM] * 4 + [pl.BlockSpec()] * 2,
        out_specs=[SMEM] + [pl.BlockSpec()] * 2,
        out_shape=[jax.ShapeDtypeStruct((16,), jnp.int32), slot, slot],
        compiler_params=PARAMS,
    )(own, enc, dec, target, keys, values)


def split_kernel(q_ref, g_ref, parts_ref):
    for j in range(parts_ref.shape[0]):
        for c, in_ref in enumerate((q_ref, g_ref)):
            parts_ref[j, c] = in_ref[:, j * HEAD_DIM : (j + 1) * HEAD_DIM]


def split(queries, grads):
    rows, width = queries.shape
    return pl.pallas_call(
        split_kernel,
        out_shape=jax.ShapeDtypeStruct((width // HEAD_DIM, 2, rows, HEAD_DIM), queries.dtype),
        compiler_params=PARAMS,
    )(queries, grads)


def join_kernel(parts_ref, *outs):
    for j in range(parts_ref.shape[0]):
        for c, out_ref in enumerate(outs):
            out_ref[:, j * HEAD_DIM : (j + 1) * HEAD_DIM] = parts_ref[j, c]


def join(parts):
    heads, count, rows, _ = parts.shape
    return pl.pallas_call(
        join_kernel,
        out_shape=[jax.ShapeDtypeStruct((rows, heads * HEAD_DIM), parts.dtype)] * count,
        compiler_params=PARAMS,
    )(parts)


def pack_kernel(scal, in_ref, xm_ref, xn_ref):
    arrays = [in_ref[:, c].reshape(-1, HEAD_DIM) for c in range(in_ref.shape[1])]
    unpacked(scal[COL], scal[DEC_LEN], scal[DEC_LEN + 1], arrays, xm_ref, xn_ref)


def pack(scal, parts, cap):
    slot = jax.ShapeDtypeStruct((parts.shape[1], cap, HEAD_DIM), parts.dtype)
    return pl.pallas_call(
        pack_kernel,
        in_specs=[SMEM, pl.BlockSpec()],
        out_shape=[slot, slot],
        compiler_params=PARAMS,
    )(scal, parts)


def merge_kernel(length, total, scal, a_ref, b_ref, *outs):
    for c in range(a_ref.shape[0]):
        rows = packed(scal[COL], scal[length], scal[length + 1], a_ref[c], b_ref[c], total)
        if len(outs) == 1:
            outs[0][:, c] = rows.reshape(outs[0].shape[0], outs[0].shape[2], HEAD_DIM)
        else:
            outs[c][...] = rows


def merge(scal, length, a, b, total, parts):
    if parts > 1:
        out = [jax.ShapeDtypeStruct((parts, a.shape[0], total // parts, HEAD_DIM), a.dtype)]
    else:
        out = [jax.ShapeDtypeStruct((total, HEAD_DIM), a.dtype)] * a.shape[0]
    return pl.pallas_call(
        functools.partial(merge_kernel, length, total),
        in_specs=[SMEM, pl.BlockSpec(), pl.BlockSpec()],
        out_shape=out,
        compiler_params=PARAMS,
    )(scal, a, b)


def attend_kernel(n, scal, x_ref, kv_ref, y_ref, dkv_ref, acc_ref):
    step = pl.program_id(0)
    rows = x_ref.shape[1]
    valid = lax.broadcasted_iota(jnp.int32, (rows, 1), 0) + step * rows < scal[QUERY_LEN + n]
    q, g, keys, values = x_ref[0], x_ref[1], kv_ref[0], kv_ref[1]
    scores = dot(q, keys, NT) * SCALING
    col = lax.broadcasted_iota(jnp.int32, (1, scores.shape[1]), 1)
    scores = jnp.where(col < scal[KEY_LEN + n], scores, -1e30)
    raised = jnp.exp(scores - jnp.max(scores, axis=1, keepdims=True))
    probs = raised * (1.0 / jnp.sum(raised, axis=1, keepdims=True))
    probs_b = probs.astype(jnp.bfloat16)
    prob_grad = dot(g, values, NT)
    row_dot = jnp.sum(probs * prob_grad, axis=1, keepdims=True)
    score_grad = (probs * (prob_grad - row_dot)).astype(jnp.bfloat16)
    y_ref[0] = jnp.where(valid, dot(probs_b, values), 0.0).astype(y_ref.dtype)
    y_ref[1] = jnp.where(valid, dot(score_grad, keys) * SCALING, 0.0).astype(y_ref.dtype)

    @pl.when(step == 0)
    def _():
        acc_ref[...] = jnp.zeros_like(acc_ref)

    acc_ref[0] += dot(score_grad, q, TN)
    acc_ref[1] += dot(probs_b, g, TN)

    @pl.when(step == pl.num_programs(0) - 1)
    def _():
        dkv_ref[0] = (acc_ref[0] * SCALING).astype(dkv_ref.dtype)
        dkv_ref[1] = acc_ref[1].astype(dkv_ref.dtype)


def attend(n, scal, x, kv):
    cap, keys = x.shape[1], kv.shape[1]
    blocks = pl.BlockSpec((2, ROWS, HEAD_DIM), lambda i: (0, i, 0))
    whole = pl.BlockSpec(kv.shape, lambda i: (0, 0, 0))
    return pl.pallas_call(
        functools.partial(attend_kernel, n),
        grid=(cap // ROWS,),
        in_specs=[SMEM, blocks, whole],
        out_specs=[blocks, whole],
        out_shape=[jax.ShapeDtypeStruct(x.shape, x.dtype), jax.ShapeDtypeStruct(kv.shape, kv.dtype)],
        scratch_shapes=[pltpu.VMEM(kv.shape, jnp.float32)],
        compiler_params=PARAMS,
        cost_estimate=pl.CostEstimate(
            flops=12 * cap * keys * HEAD_DIM, bytes_accessed=3 * 2**20, transcendentals=cap * keys
        ),
    )(scal, x, kv)


def exchanged(parts, flag):
    def swap(parts):
        return lax.all_to_all(parts, "mp", split_axis=0, concat_axis=0, tiled=True)

    return lax.cond(flag, swap, lambda parts: parts, parts)


def local(
    queries,
    encoder_keys,
    encoder_values,
    context_grad,
    encoder_lengths,
    decoder_lengths,
    target_device,
):
    owners = lax.axis_size("dp")
    own = lax.axis_index("dp").astype(jnp.int32).reshape(1)
    seq_count = target_device.shape[1]
    dec_total = queries.shape[0] * lax.axis_size("mp")
    dec_cap = dec_total // seq_count
    enc_total = encoder_keys.shape[0]
    enc_cap = enc_total // seq_count
    scal, kvm, kvn = prepare(
        own, encoder_lengths.T, decoder_lengths.T, target_device.T, encoder_keys, encoder_values, owners, enc_cap
    )
    way, around = scal[WAY], scal[AROUND]
    ways = [
        (RING * i + min(j, KEY_HOPS), RING * i + min(j + 1, KEY_HOPS))
        for i in range(owners // RING)
        for j in range(KEY_HOPS + 1)
    ]
    rest = [(max(j - KEY_HOPS, 0), j + 1 - KEY_HOPS) for j in range(KEY_HOPS - 1, RING // 2)]

    def queries_out(m, n):
        def run(xm, xn):
            xn = passed_along(xn, n)
            return xn, passed_along(xm, -m)

        return run

    def out_along(m, n, last):
        def run(scal, around, kvm, kvn, queries, context_grad):
            kvn = passed_along(kvn, -n)
            kvm = passed_along(kvm, m)
            xm, xn = pack(scal, exchanged(split(queries, context_grad), around >= 0), dec_cap)
            if last:
                xn, xm = lax.switch(around, [queries_out(*r) for r in rest], xm, xn)
            return kvn, kvm, xn, xm

        return run

    kvn, kvm, xn, xm = lax.switch(
        way,
        [out_along(*w, i % (KEY_HOPS + 1) == KEY_HOPS) for i, w in enumerate(ways)],
        scal, around, kvm, kvn, queries, context_grad,
    )

    def queries_back(m, n):
        def run(scal, xm, xn, kvm, kvn):
            yn, kvn = attend(1, scal, xn, kvn)
            yn = passed_along(yn, -n)
            ym, kvm = attend(0, scal, xm, kvm)
            return yn, passed_along(ym, m), kvn, kvm

        return run

    yn, ym, kvn, kvm = lax.switch(around, [queries_back(*r) for r in rest], scal, xm, xn, kvm, kvn)

    def back_along(m, n):
        def run(scal, around, kvm, kvn, ym, yn):
            kvn = passed_along(kvn, n)
            kvm = passed_along(kvm, -m)
            (parts,) = merge(scal, DEC_LEN, ym, yn, dec_total, lax.axis_size("mp"))
            return kvn, kvm, *join(exchanged(parts, around >= 0))

        return run

    kvn, kvm, context, query_grad = lax.switch(
        way, [back_along(*w) for w in ways], scal, around, kvm, kvn, ym, yn
    )
    key_grad, value_grad = merge(scal, ENC_LEN, kvm, kvn, enc_total, 1)
    return (context, query_grad, key_grad, value_grad)


def solution(mesh):
    return jax.shard_map(
        local,
        mesh=mesh,
        in_specs=(
            P(("dp", "mp"), None),
            P("dp", "mp"),
            P("dp", "mp"),
            P(("dp", "mp"), None),
            P(),
            P(),
            P(),
        ),
        out_specs=(P(("dp", "mp"), None), P(("dp", "mp"), None), P("dp", "mp"), P("dp", "mp")),
        check_vma=False,
    )
```

```python
import functools

import jax
import jax.numpy as jnp
from jax import lax
from jax.experimental import pallas as pl
from jax.experimental.pallas import tpu as pltpu
from jax.sharding import PartitionSpec as P

HEAD_DIM = 256
SCALING = HEAD_DIM ** (-0.5)
ROWS = 256
RING = 16
KEY_HOPS = 2
SMEM = pl.BlockSpec(memory_space=pltpu.SMEM)
NT = (((1,), (1,)), ((), ()))
TN = (((0,), (0,)), ((), ()))
WAY, AROUND, COL, DEC_LEN, ENC_LEN, KEY_LEN, QUERY_LEN = 0, 1, 2, 4, 6, 8, 10
PARAMS = pltpu.CompilerParams(vmem_limit_bytes=32 * 2**20)


def dot(a, b, dims=(((1,), (0,)), ((), ()))):
    return lax.dot_general(a, b, dims, preferred_element_type=jnp.float32)


def passed_along(block, distance):
    owners = lax.axis_size("dp")
    if distance % owners == 0:
        return block
    return lax.ppermute(block, "dp", [(i, (i + distance) % owners) for i in range(owners)])


def one_hot(shape, gap, live):
    row = lax.broadcasted_iota(jnp.int32, shape, 0)
    col = lax.broadcasted_iota(jnp.int32, shape, 1)
    return ((col - row == gap) & (col < live)).astype(jnp.float32).astype(jnp.bfloat16)


def unpacked(m, len0, len1, arrays, m_ref, n_ref):
    total, cap = arrays[0].shape[0], m_ref.shape[1]
    pick = one_hot((cap, total), len0, len0 + len1)
    live = lax.broadcasted_iota(jnp.int32, (cap, 1), 0) < len0
    for c, rows in enumerate(arrays):
        first = jnp.where(live, rows[:cap], jnp.zeros_like(rows[:cap]))
        second = dot(pick, rows).astype(rows.dtype)
        m_ref[c] = jnp.where(m == 0, first, second)
        n_ref[c] = jnp.where(m == 0, second, first)


def packed(m, len0, len1, a, b, total):
    cap = a.shape[0]
    first = jnp.where(m == 0, a, b)
    second = jnp.where(m == 0, b, a)
    live = lax.broadcasted_iota(jnp.int32, (cap, 1), 0) < len0
    first = jnp.where(live, first, jnp.zeros_like(first)).astype(jnp.float32)
    moved = dot(one_hot((total, cap), -len0, len1), second)
    return jnp.concatenate([moved[:cap] + first, moved[cap:]], axis=0).astype(a.dtype)


def prepare_kernel(owners, own_ref, enc_ref, dec_ref, target_ref, k_ref, v_ref, out_ref, kvm_ref, kvn_ref):
    own = own_ref[0]
    shift0 = lax.rem(target_ref[0, 0], owners)
    m = jnp.where(lax.rem(shift0, RING) < RING // 2, 0, 1)
    shift = jnp.where(m == 0, shift0, owners - 1 - shift0)
    h = lax.rem(shift, RING)
    k = lax.div(shift, RING)
    out_ref[WAY] = k * (KEY_HOPS + 1) + jnp.minimum(h, KEY_HOPS) - 1
    out_ref[AROUND] = jnp.maximum(h, KEY_HOPS - 1) - (KEY_HOPS - 1)
    out_ref[COL] = m
    out_ref[COL + 1] = 0

    def wrapped(i):
        return lax.rem(i + 2 * owners, owners)

    for n in range(2):
        col = m if n == 0 else 1 - m
        sign = 1 - 2 * n
        hops = jnp.minimum(h + n, KEY_HOPS)
        out_ref[DEC_LEN + n] = dec_ref[n, own]
        out_ref[ENC_LEN + n] = enc_ref[n, own]
        out_ref[KEY_LEN + n] = enc_ref[col, wrapped(own - sign * (RING * k + hops))]
        out_ref[QUERY_LEN + n] = dec_ref[col, wrapped(own + sign * (h + n - hops))]
    for n in range(QUERY_LEN + 2, out_ref.shape[0]):
        out_ref[n] = 0
    unpacked(m, enc_ref[0, own], enc_ref[1, own], (k_ref[...], v_ref[...]), kvm_ref, kvn_ref)


def prepare(own, enc, dec, target, keys, values, owners, cap):
    slot = jax.ShapeDtypeStruct((2, cap, HEAD_DIM), keys.dtype)
    return pl.pallas_call(
        functools.partial(prepare_kernel, owners),
        in_specs=[SMEM] * 4 + [pl.BlockSpec()] * 2,
        out_specs=[SMEM] + [pl.BlockSpec()] * 2,
        out_shape=[jax.ShapeDtypeStruct((16,), jnp.int32), slot, slot],
        compiler_params=PARAMS,
    )(own, enc, dec, target, keys, values)


def split_kernel(q_ref, g_ref, parts_ref):
    for j in range(parts_ref.shape[0]):
        for c, in_ref in enumerate((q_ref, g_ref)):
            parts_ref[j, c] = in_ref[:, j * HEAD_DIM : (j + 1) * HEAD_DIM]


def split(queries, grads):
    rows, width = queries.shape
    return pl.pallas_call(
        split_kernel,
        out_shape=jax.ShapeDtypeStruct((width // HEAD_DIM, 2, rows, HEAD_DIM), queries.dtype),
        compiler_params=PARAMS,
    )(queries, grads)


def join_kernel(parts_ref, *outs):
    for j in range(parts_ref.shape[0]):
        for c, out_ref in enumerate(outs):
            out_ref[:, j * HEAD_DIM : (j + 1) * HEAD_DIM] = parts_ref[j, c]


def join(parts):
    heads, count, rows, _ = parts.shape
    return pl.pallas_call(
        join_kernel,
        out_shape=[jax.ShapeDtypeStruct((rows, heads * HEAD_DIM), parts.dtype)] * count,
        compiler_params=PARAMS,
    )(parts)


def pack_kernel(scal, in_ref, xm_ref, xn_ref):
    size, count, rows, _ = in_ref.shape
    m, len0, len1 = scal[COL], scal[DEC_LEN], scal[DEC_LEN + 1]

    def part(j, _):
        base = pl.multiple_of(j * rows, rows)
        at = pl.ds(base, rows)
        pick = one_hot((rows, size * rows), len0 + base, len0 + len1)
        live = lax.broadcasted_iota(jnp.int32, (rows, 1), 0) + base < len0
        for c in range(count):
            first = in_ref[j, c]
            first = jnp.where(live, first, jnp.zeros_like(first))
            second = dot(pick, in_ref[:, c].reshape(size * rows, HEAD_DIM)).astype(first.dtype)
            xm_ref[c, at, :] = jnp.where(m == 0, first, second)
            xn_ref[c, at, :] = jnp.where(m == 0, second, first)
        return 0

    lax.fori_loop(0, xm_ref.shape[1] // rows, part, 0)


def pack(scal, parts, cap):
    slot = jax.ShapeDtypeStruct((parts.shape[1], cap, HEAD_DIM), parts.dtype)
    return pl.pallas_call(
        pack_kernel,
        in_specs=[SMEM, pl.BlockSpec()],
        out_shape=[slot, slot],
        compiler_params=PARAMS,
    )(scal, parts)


def merge_parts_kernel(scal, a_ref, b_ref, parts_ref):
    size, count, rows, _ = parts_ref.shape
    cap = a_ref.shape[1]
    m, len0, len1 = scal[COL], scal[DEC_LEN], scal[DEC_LEN + 1]

    def part(j, _):
        base = j * rows
        at = pl.ds(pl.multiple_of(jnp.minimum(base, cap - rows), rows), rows)
        live = lax.broadcasted_iota(jnp.int32, (rows, 1), 0) + base < len0
        pick = one_hot((rows, cap), -len0 + base, len1)
        for c in range(count):
            first = jnp.where(m == 0, a_ref[c, at, :], b_ref[c, at, :])
            second = jnp.where(m == 0, b_ref[c], a_ref[c])
            first = jnp.where(live, first, jnp.zeros_like(first)).astype(jnp.float32)
            parts_ref[j, c] = (dot(pick, second) + first).astype(parts_ref.dtype)
        return 0

    lax.fori_loop(0, size, part, 0)


def merge_parts(scal, a, b, parts):
    rows = a.shape[1] * 2 // parts
    return pl.pallas_call(
        merge_parts_kernel,
        in_specs=[SMEM, pl.BlockSpec(), pl.BlockSpec()],
        out_shape=jax.ShapeDtypeStruct((parts, a.shape[0], rows, HEAD_DIM), a.dtype),
        compiler_params=PARAMS,
    )(scal, a, b)


def merge_keys_kernel(scal, a_ref, b_ref, *outs):
    for c, out_ref in enumerate(outs):
        rows = packed(scal[COL], scal[ENC_LEN], scal[ENC_LEN + 1], a_ref[c], b_ref[c], out_ref.shape[0])
        out_ref[...] = rows


def merge_keys(scal, a, b, total):
    return pl.pallas_call(
        merge_keys_kernel,
        in_specs=[SMEM, pl.BlockSpec(), pl.BlockSpec()],
        out_shape=[jax.ShapeDtypeStruct((total, HEAD_DIM), a.dtype)] * a.shape[0],
        compiler_params=PARAMS,
    )(scal, a, b)


def attend_kernel(n, scal, x_ref, kv_ref, y_ref, dkv_ref, acc_ref):
    step = pl.program_id(0)
    rows = x_ref.shape[1]
    valid = lax.broadcasted_iota(jnp.int32, (rows, 1), 0) + step * rows < scal[QUERY_LEN + n]
    q, g, keys, values = x_ref[0], x_ref[1], kv_ref[0], kv_ref[1]
    scores = dot(q, keys, NT) * SCALING
    col = lax.broadcasted_iota(jnp.int32, (1, scores.shape[1]), 1)
    scores = jnp.where(col < scal[KEY_LEN + n], scores, -1e30)
    raised = jnp.exp(scores - jnp.max(scores, axis=1, keepdims=True))
    probs = raised * (1.0 / jnp.sum(raised, axis=1, keepdims=True))
    probs_b = probs.astype(jnp.bfloat16)
    prob_grad = dot(g, values, NT)
    row_dot = jnp.sum(probs * prob_grad, axis=1, keepdims=True)
    score_grad = (probs * (prob_grad - row_dot)).astype(jnp.bfloat16)
    y_ref[0] = jnp.where(valid, dot(probs_b, values), 0.0).astype(y_ref.dtype)
    y_ref[1] = jnp.where(valid, dot(score_grad, keys) * SCALING, 0.0).astype(y_ref.dtype)

    @pl.when(step == 0)
    def _():
        acc_ref[...] = jnp.zeros_like(acc_ref)

    acc_ref[0] += dot(score_grad, q, TN)
    acc_ref[1] += dot(probs_b, g, TN)

    @pl.when(step == pl.num_programs(0) - 1)
    def _():
        dkv_ref[0] = (acc_ref[0] * SCALING).astype(dkv_ref.dtype)
        dkv_ref[1] = acc_ref[1].astype(dkv_ref.dtype)


def attend(n, scal, x, kv):
    cap, keys = x.shape[1], kv.shape[1]
    blocks = pl.BlockSpec((2, ROWS, HEAD_DIM), lambda i: (0, i, 0))
    whole = pl.BlockSpec(kv.shape, lambda i: (0, 0, 0))
    return pl.pallas_call(
        functools.partial(attend_kernel, n),
        grid=(cap // ROWS,),
        in_specs=[SMEM, blocks, whole],
        out_specs=[blocks, whole],
        out_shape=[jax.ShapeDtypeStruct(x.shape, x.dtype), jax.ShapeDtypeStruct(kv.shape, kv.dtype)],
        scratch_shapes=[pltpu.VMEM(kv.shape, jnp.float32)],
        compiler_params=PARAMS,
        cost_estimate=pl.CostEstimate(
            flops=12 * cap * keys * HEAD_DIM, bytes_accessed=3 * 2**20, transcendentals=cap * keys
        ),
    )(scal, x, kv)


def exchanged(parts, flag):
    def swap(parts):
        return lax.all_to_all(parts, "mp", split_axis=0, concat_axis=0, tiled=True)

    return lax.cond(flag, swap, lambda parts: parts, parts)


def local(
    queries,
    encoder_keys,
    encoder_values,
    context_grad,
    encoder_lengths,
    decoder_lengths,
    target_device,
):
    owners = lax.axis_size("dp")
    own = lax.axis_index("dp").astype(jnp.int32).reshape(1)
    seq_count = target_device.shape[1]
    dec_total = queries.shape[0] * lax.axis_size("mp")
    dec_cap = dec_total // seq_count
    enc_total = encoder_keys.shape[0]
    enc_cap = enc_total // seq_count
    scal, kvm, kvn = prepare(
        own, encoder_lengths.T, decoder_lengths.T, target_device.T, encoder_keys, encoder_values, owners, enc_cap
    )
    way, around = scal[WAY], scal[AROUND]
    ways = [
        (RING * i + min(j, KEY_HOPS), RING * i + min(j + 1, KEY_HOPS))
        for i in range(owners // RING)
        for j in range(KEY_HOPS + 1)
    ][1:]
    rest = [(max(j - KEY_HOPS, 0), j + 1 - KEY_HOPS) for j in range(KEY_HOPS - 1, RING // 2)]

    def queries_out(m, n):
        def run(xm, xn):
            xn = passed_along(xn, n)
            return xn, passed_along(xm, -m)

        return run

    def out_along(m, n, last):
        def run(scal, around, kvm, kvn, queries, context_grad):
            kvn = passed_along(kvn, -n)
            kvm = passed_along(kvm, m)
            xm, xn = pack(scal, exchanged(split(queries, context_grad), around >= 0), dec_cap)
            if last:
                xn, xm = lax.switch(around, [queries_out(*r) for r in rest], xm, xn)
            return kvn, kvm, xn, xm

        return run

    kvn, kvm, xn, xm = lax.switch(
        way,
        [out_along(*w, i % (KEY_HOPS + 1) == KEY_HOPS - 1) for i, w in enumerate(ways)],
        scal, around, kvm, kvn, queries, context_grad,
    )

    def queries_back(m, n):
        def run(ym, yn):
            yn = passed_along(yn, -n)
            return yn, passed_along(ym, m)

        return run

    yn, kvn = attend(1, scal, xn, kvn)
    ym, kvm = attend(0, scal, xm, kvm)
    yn, ym = lax.switch(around, [queries_back(*r) for r in rest], ym, yn)

    def back_along(m, n):
        def run(scal, around, kvm, kvn, ym, yn):
            kvn = passed_along(kvn, n)
            kvm = passed_along(kvm, -m)
            parts = merge_parts(scal, ym, yn, lax.axis_size("mp"))
            return kvn, kvm, *join(exchanged(parts, around >= 0))

        return run

    kvn, kvm, context, query_grad = lax.switch(
        way, [back_along(*w) for w in ways], scal, around, kvm, kvn, ym, yn
    )
    key_grad, value_grad = merge_keys(scal, kvm, kvn, enc_total)
    return (context, query_grad, key_grad, value_grad)


def solution(mesh):
    return jax.shard_map(
        local,
        mesh=mesh,
        in_specs=(
            P(("dp", "mp"), None),
            P("dp", "mp"),
            P("dp", "mp"),
            P(("dp", "mp"), None),
            P(),
            P(),
            P(),
        ),
        out_specs=(P(("dp", "mp"), None), P(("dp", "mp"), None), P("dp", "mp"), P("dp", "mp")),
        check_vma=False,
    )
```

```python
import functools

import jax
import jax.numpy as jnp
from jax import lax
from jax.experimental import pallas as pl
from jax.experimental.pallas import tpu as pltpu
from jax.sharding import PartitionSpec as P

HEAD_DIM = 256
SCALING = HEAD_DIM ** (-0.5)
ROWS = 256
RING = 16
KEY_HOPS = 2
SMEM = pl.BlockSpec(memory_space=pltpu.SMEM)
NT = (((1,), (1,)), ((), ()))
TN = (((0,), (0,)), ((), ()))
WAY, AROUND, COL, DEC_LEN, ENC_LEN, KEY_LEN, QUERY_LEN = 0, 1, 2, 4, 6, 8, 10
PARAMS = pltpu.CompilerParams(vmem_limit_bytes=32 * 2**20)
WIDE = pltpu.CompilerParams(vmem_limit_bytes=60 * 2**20)


def dot(a, b, dims=(((1,), (0,)), ((), ()))):
    return lax.dot_general(a, b, dims, preferred_element_type=jnp.float32)


def passed_along(block, distance):
    owners = lax.axis_size("dp")
    if distance % owners == 0:
        return block
    return lax.ppermute(block, "dp", [(i, (i + distance) % owners) for i in range(owners)])


def one_hot(shape, gap, live):
    row = lax.broadcasted_iota(jnp.int32, shape, 0)
    col = lax.broadcasted_iota(jnp.int32, shape, 1)
    return ((col - row == gap) & (col < live)).astype(jnp.float32).astype(jnp.bfloat16)


def unpacked(m, len0, len1, arrays, m_ref, n_ref):
    total, cap = arrays[0].shape[0], m_ref.shape[1]
    pick = one_hot((cap, total), len0, len0 + len1)
    live = lax.broadcasted_iota(jnp.int32, (cap, 1), 0) < len0
    for c, rows in enumerate(arrays):
        first = jnp.where(live, rows[:cap], jnp.zeros_like(rows[:cap]))
        second = dot(pick, rows).astype(rows.dtype)
        m_ref[c] = jnp.where(m == 0, first, second)
        n_ref[c] = jnp.where(m == 0, second, first)


def prepare_kernel(
    owners, own_ref, enc_ref, dec_ref, target_ref, k_hbm, v_hbm, out_ref, kvm_ref, kvn_ref, k_ref, v_ref, sems
):
    copies = [
        pltpu.make_async_copy(k_hbm, k_ref, sems.at[0]),
        pltpu.make_async_copy(v_hbm, v_ref, sems.at[1]),
    ]
    for copy in copies:
        copy.start()
    own = own_ref[0]
    shift0 = lax.rem(target_ref[0, 0], owners)
    m = jnp.where(lax.rem(shift0, RING) < RING // 2, 0, 1)
    shift = jnp.where(m == 0, shift0, owners - 1 - shift0)
    h = lax.rem(shift, RING)
    k = lax.div(shift, RING)
    out_ref[WAY] = k * (KEY_HOPS + 1) + jnp.minimum(h, KEY_HOPS) - 1
    out_ref[AROUND] = jnp.maximum(h, KEY_HOPS - 1) - (KEY_HOPS - 1)
    out_ref[COL] = m
    out_ref[COL + 1] = 0

    def wrapped(i):
        return lax.rem(i + 2 * owners, owners)

    for n in range(2):
        col = m if n == 0 else 1 - m
        sign = 1 - 2 * n
        hops = jnp.minimum(h + n, KEY_HOPS)
        out_ref[DEC_LEN + n] = dec_ref[n, own]
        out_ref[ENC_LEN + n] = enc_ref[n, own]
        out_ref[KEY_LEN + n] = enc_ref[col, wrapped(own - sign * (RING * k + hops))]
        out_ref[QUERY_LEN + n] = dec_ref[col, wrapped(own + sign * (h + n - hops))]
    for n in range(QUERY_LEN + 2, out_ref.shape[0]):
        out_ref[n] = 0
    for copy in copies:
        copy.wait()
    unpacked(m, enc_ref[0, own], enc_ref[1, own], (k_ref[...], v_ref[...]), kvm_ref, kvn_ref)


def prepare(own, enc, dec, target, keys, values, owners, cap):
    slot = jax.ShapeDtypeStruct((2, cap, HEAD_DIM), keys.dtype)
    return pl.pallas_call(
        functools.partial(prepare_kernel, owners),
        in_specs=[SMEM] * 4 + [pl.BlockSpec(memory_space=pl.ANY)] * 2,
        out_specs=[SMEM] + [pl.BlockSpec()] * 2,
        out_shape=[jax.ShapeDtypeStruct((16,), jnp.int32), slot, slot],
        scratch_shapes=[pltpu.VMEM(keys.shape, keys.dtype)] * 2 + [pltpu.SemaphoreType.DMA((2,))],
        compiler_params=WIDE,
    )(own, enc, dec, target, keys, values)


def split_kernel(q_ref, g_ref, parts_ref):
    for j in range(parts_ref.shape[0]):
        for c, in_ref in enumerate((q_ref, g_ref)):
            parts_ref[j, c] = in_ref[:, j * HEAD_DIM : (j + 1) * HEAD_DIM]


def split(queries, grads):
    rows, width = queries.shape
    return pl.pallas_call(
        split_kernel,
        out_shape=jax.ShapeDtypeStruct((width // HEAD_DIM, 2, rows, HEAD_DIM), queries.dtype),
        compiler_params=PARAMS,
    )(queries, grads)


def join_kernel(parts_ref, *outs):
    for j in range(parts_ref.shape[0]):
        for c, out_ref in enumerate(outs):
            out_ref[:, j * HEAD_DIM : (j + 1) * HEAD_DIM] = parts_ref[j, c]


def join(parts):
    heads, count, rows, _ = parts.shape
    return pl.pallas_call(
        join_kernel,
        out_shape=[jax.ShapeDtypeStruct((rows, heads * HEAD_DIM), parts.dtype)] * count,
        compiler_params=PARAMS,
    )(parts)


def pack_kernel(scal, in_ref, xm_ref, xn_ref):
    size, count, rows, _ = in_ref.shape
    m, len0, len1 = scal[COL], scal[DEC_LEN], scal[DEC_LEN + 1]

    def part(j, _):
        base = pl.multiple_of(j * rows, rows)
        at = pl.ds(base, rows)
        pick = one_hot((rows, size * rows), len0 + base, len0 + len1)
        live = lax.broadcasted_iota(jnp.int32, (rows, 1), 0) + base < len0
        for c in range(count):
            first = in_ref[j, c]
            first = jnp.where(live, first, jnp.zeros_like(first))
            second = dot(pick, in_ref[:, c].reshape(size * rows, HEAD_DIM)).astype(first.dtype)
            xm_ref[c, at, :] = jnp.where(m == 0, first, second)
            xn_ref[c, at, :] = jnp.where(m == 0, second, first)
        return 0

    lax.fori_loop(0, xm_ref.shape[1] // rows, part, 0)


def pack(scal, parts, cap):
    slot = jax.ShapeDtypeStruct((parts.shape[1], cap, HEAD_DIM), parts.dtype)
    return pl.pallas_call(
        pack_kernel,
        in_specs=[SMEM, pl.BlockSpec()],
        out_shape=[slot, slot],
        compiler_params=PARAMS,
    )(scal, parts)


def merge_parts_kernel(scal, a_ref, b_ref, parts_ref):
    size, count, rows, _ = parts_ref.shape
    cap = a_ref.shape[1]
    m, len0, len1 = scal[COL], scal[DEC_LEN], scal[DEC_LEN + 1]

    def part(j, _):
        base = j * rows
        at = pl.ds(pl.multiple_of(jnp.minimum(base, cap - rows), rows), rows)
        live = lax.broadcasted_iota(jnp.int32, (rows, 1), 0) + base < len0
        pick = one_hot((rows, cap), -len0 + base, len1)
        for c in range(count):
            first = jnp.where(m == 0, a_ref[c, at, :], b_ref[c, at, :])
            second = jnp.where(m == 0, b_ref[c], a_ref[c])
            first = jnp.where(live, first, jnp.zeros_like(first)).astype(jnp.float32)
            parts_ref[j, c] = (dot(pick, second) + first).astype(parts_ref.dtype)
        return 0

    lax.fori_loop(0, size, part, 0)


def merge_parts(scal, a, b, parts):
    rows = a.shape[1] * 2 // parts
    return pl.pallas_call(
        merge_parts_kernel,
        in_specs=[SMEM, pl.BlockSpec(), pl.BlockSpec()],
        out_shape=jax.ShapeDtypeStruct((parts, a.shape[0], rows, HEAD_DIM), a.dtype),
        compiler_params=PARAMS,
    )(scal, a, b)


def merge_keys_kernel(scal, a_hbm, b_hbm, dk_hbm, dv_hbm, a_ref, b_ref, out_ref, sems):
    count, cap, _ = a_ref.shape
    total = out_ref.shape[1]
    ins = [
        [pltpu.make_async_copy(src.at[c], dst.at[c], sems.at[i, c]) for i, (src, dst) in enumerate(pairs)]
        for c, pairs in enumerate([((a_hbm, a_ref), (b_hbm, b_ref))] * count)
    ]
    outs = [pltpu.make_async_copy(out_ref.at[c], dst, sems.at[2, c]) for c, dst in enumerate((dk_hbm, dv_hbm))]
    for copies in ins:
        for copy in copies:
            copy.start()
    m, len0, len1 = scal[COL], scal[ENC_LEN], scal[ENC_LEN + 1]
    low = cap // 2
    pick = one_hot((total - low, cap), low - len0, len1)
    live = lax.broadcasted_iota(jnp.int32, (cap, 1), 0) < len0
    for c in range(count):
        for copy in ins[c]:
            copy.wait()
        first = jnp.where(m == 0, a_ref[c], b_ref[c])
        second = jnp.where(m == 0, b_ref[c], a_ref[c])
        first = jnp.where(live, first, jnp.zeros_like(first)).astype(jnp.float32)
        moved = dot(pick, second)
        out_ref[c, :low] = first[:low].astype(out_ref.dtype)
        out_ref[c, low:cap] = (moved[: cap - low] + first[low:]).astype(out_ref.dtype)
        out_ref[c, cap:] = moved[cap - low :].astype(out_ref.dtype)
        outs[c].start()
    for copy in outs:
        copy.wait()


def merge_keys(scal, a, b, total):
    hbm = pl.BlockSpec(memory_space=pl.ANY)
    return pl.pallas_call(
        merge_keys_kernel,
        in_specs=[SMEM, hbm, hbm],
        out_specs=[hbm, hbm],
        out_shape=[jax.ShapeDtypeStruct((total, HEAD_DIM), a.dtype)] * a.shape[0],
        scratch_shapes=[
            pltpu.VMEM(a.shape, a.dtype),
            pltpu.VMEM(b.shape, b.dtype),
            pltpu.VMEM((a.shape[0], total, HEAD_DIM), a.dtype),
            pltpu.SemaphoreType.DMA((3, a.shape[0])),
        ],
        compiler_params=WIDE,
    )(scal, a, b)


def attend_rows(q, g, keys, values, key_len, valid):
    scores = dot(q, keys, NT) * SCALING
    col = lax.broadcasted_iota(jnp.int32, (1, scores.shape[1]), 1)
    scores = jnp.where(col < key_len, scores, -1e30)
    raised = jnp.exp(scores - jnp.max(scores, axis=1, keepdims=True))
    probs = raised * (1.0 / jnp.sum(raised, axis=1, keepdims=True))
    probs_b = probs.astype(jnp.bfloat16)
    prob_grad = dot(g, values, NT)
    row_dot = jnp.sum(probs * prob_grad, axis=1, keepdims=True)
    score_grad = (probs * (prob_grad - row_dot)).astype(jnp.bfloat16)
    context = jnp.where(valid, dot(probs_b, values), 0.0).astype(jnp.bfloat16)
    query_grad = jnp.where(valid, dot(score_grad, keys) * SCALING, 0.0).astype(jnp.bfloat16)
    return context, query_grad, probs_b, score_grad


def attend_kernel(scal, xm_ref, xn_ref, kvm_ref, kvn_ref, ym_ref, yn_ref, dkvm_ref, dkvn_ref):
    columns = ((xm_ref, kvm_ref, ym_ref, dkvm_ref), (xn_ref, kvn_ref, yn_ref, dkvn_ref))
    for n, (x_ref, kv_ref, y_ref, dkv_ref) in enumerate(columns):
        probs, score_grads = [], []
        for base in range(0, x_ref.shape[1], ROWS):
            at = slice(base, base + ROWS)
            valid = lax.broadcasted_iota(jnp.int32, (ROWS, 1), 0) + base < scal[QUERY_LEN + n]
            y_ref[0, at], y_ref[1, at], probs_b, score_grad = attend_rows(
                x_ref[0, at], x_ref[1, at], kv_ref[0], kv_ref[1], scal[KEY_LEN + n], valid
            )
            probs.append(probs_b)
            score_grads.append(score_grad)
        key_grad = dot(jnp.concatenate(score_grads), x_ref[0], TN) * SCALING
        dkv_ref[0] = key_grad.astype(dkv_ref.dtype)
        dkv_ref[1] = dot(jnp.concatenate(probs), x_ref[1], TN).astype(dkv_ref.dtype)


def attend(scal, xm, xn, kvm, kvn):
    cap, keys = xm.shape[1], kvm.shape[1]
    return pl.pallas_call(
        attend_kernel,
        in_specs=[SMEM] + [pl.BlockSpec()] * 4,
        out_shape=[jax.ShapeDtypeStruct(a.shape, a.dtype) for a in (xm, xn, kvm, kvn)],
        compiler_params=PARAMS,
        cost_estimate=pl.CostEstimate(
            flops=24 * cap * keys * HEAD_DIM, bytes_accessed=5 * 2**20, transcendentals=2 * cap * keys
        ),
    )(scal, xm, xn, kvm, kvn)


def exchanged(parts, flag):
    def swap(parts):
        return lax.all_to_all(parts, "mp", split_axis=0, concat_axis=0, tiled=True)

    return lax.cond(flag, swap, lambda parts: parts, parts)


def local(
    queries,
    encoder_keys,
    encoder_values,
    context_grad,
    encoder_lengths,
    decoder_lengths,
    target_device,
):
    owners = lax.axis_size("dp")
    own = lax.axis_index("dp").astype(jnp.int32).reshape(1)
    seq_count = target_device.shape[1]
    dec_total = queries.shape[0] * lax.axis_size("mp")
    dec_cap = dec_total // seq_count
    enc_total = encoder_keys.shape[0]
    enc_cap = enc_total // seq_count
    scal, kvm, kvn = prepare(
        own, encoder_lengths.T, decoder_lengths.T, target_device.T, encoder_keys, encoder_values, owners, enc_cap
    )
    way, around = scal[WAY], scal[AROUND]
    ways = [
        (RING * i + min(j, KEY_HOPS), RING * i + min(j + 1, KEY_HOPS))
        for i in range(owners // RING)
        for j in range(KEY_HOPS + 1)
    ][1:]
    rest = [(max(j - KEY_HOPS, 0), j + 1 - KEY_HOPS) for j in range(KEY_HOPS - 1, RING // 2)]

    def queries_out(m, n):
        def run(xm, xn):
            xn = passed_along(xn, n)
            return xn, passed_along(xm, -m)

        return run

    def out_along(m, n, last):
        def run(scal, around, kvm, kvn, queries, context_grad):
            kvn = passed_along(kvn, -n)
            kvm = passed_along(kvm, m)
            xm, xn = pack(scal, exchanged(split(queries, context_grad), around >= 0), dec_cap)
            if last:
                xn, xm = lax.switch(around, [queries_out(*r) for r in rest], xm, xn)
            return kvn, kvm, xn, xm

        return run

    kvn, kvm, xn, xm = lax.switch(
        way,
        [out_along(*w, i % (KEY_HOPS + 1) == KEY_HOPS - 1) for i, w in enumerate(ways)],
        scal, around, kvm, kvn, queries, context_grad,
    )

    def queries_back(m, n):
        def run(ym, yn):
            yn = passed_along(yn, -n)
            return yn, passed_along(ym, m)

        return run

    ym, yn, kvm, kvn = attend(scal, xm, xn, kvm, kvn)
    yn, ym = lax.switch(around, [queries_back(*r) for r in rest], ym, yn)

    def back_along(m, n):
        def run(scal, around, kvm, kvn, ym, yn):
            kvn = passed_along(kvn, n)
            kvm = passed_along(kvm, -m)
            parts = merge_parts(scal, ym, yn, lax.axis_size("mp"))
            return kvn, kvm, *join(exchanged(parts, around >= 0))

        return run

    kvn, kvm, context, query_grad = lax.switch(
        way, [back_along(*w) for w in ways], scal, around, kvm, kvn, ym, yn
    )
    key_grad, value_grad = merge_keys(scal, kvm, kvn, enc_total)
    return (context, query_grad, key_grad, value_grad)


def solution(mesh):
    return jax.shard_map(
        local,
        mesh=mesh,
        in_specs=(
            P(("dp", "mp"), None),
            P("dp", "mp"),
            P("dp", "mp"),
            P(("dp", "mp"), None),
            P(),
            P(),
            P(),
        ),
        out_specs=(P(("dp", "mp"), None), P(("dp", "mp"), None), P("dp", "mp"), P("dp", "mp")),
        check_vma=False,
    )
```

```python
import functools

import jax
import jax.numpy as jnp
from jax import lax
from jax.experimental import pallas as pl
from jax.experimental.pallas import tpu as pltpu
from jax.sharding import PartitionSpec as P

HEAD_DIM = 256
SCALING = HEAD_DIM ** (-0.5)
ROWS = 256
RING = 16
KEY_HOPS = 2
SMEM = pl.BlockSpec(memory_space=pltpu.SMEM)
NT = (((1,), (1,)), ((), ()))
TN = (((0,), (0,)), ((), ()))
WAY, AROUND, COL, DEC_LEN, ENC_LEN, KEY_LEN, QUERY_LEN = 0, 1, 2, 4, 6, 8, 10
PARAMS = pltpu.CompilerParams(vmem_limit_bytes=32 * 2**20)
WIDE = pltpu.CompilerParams(vmem_limit_bytes=60 * 2**20)


def dot(a, b, dims=(((1,), (0,)), ((), ()))):
    return lax.dot_general(a, b, dims, preferred_element_type=jnp.float32)


def passed_along(block, distance):
    owners = lax.axis_size("dp")
    if distance % owners == 0:
        return block
    return lax.ppermute(block, "dp", [(i, (i + distance) % owners) for i in range(owners)])


def copy_kernel(in_ref, out_ref):
    out_ref[...] = in_ref[...]


def queries_along(block, distance):
    if distance:
        return passed_along(block, distance)
    return pl.pallas_call(
        copy_kernel,
        out_shape=jax.ShapeDtypeStruct(block.shape, block.dtype),
        compiler_params=PARAMS,
    )(block)


def one_hot(shape, gap):
    row = lax.broadcasted_iota(jnp.int32, shape, 0)
    col = lax.broadcasted_iota(jnp.int32, shape, 1)
    return (col - row == gap).astype(jnp.float32).astype(jnp.bfloat16)


def prepare_kernel(
    owners, own_ref, enc_ref, dec_ref, target_ref, k_hbm, v_hbm, out_ref, kvm_ref, kvn_ref, k_ref, v_ref, sems
):
    copies = [
        pltpu.make_async_copy(k_hbm, k_ref, sems.at[0]),
        pltpu.make_async_copy(v_hbm, v_ref, sems.at[1]),
    ]
    for copy in copies:
        copy.start()
    own = own_ref[0]
    shift0 = lax.rem(target_ref[0, 0], owners)
    m = jnp.where(lax.rem(shift0, RING) < RING // 2, 0, 1)
    shift = jnp.where(m == 0, shift0, owners - 1 - shift0)
    h = lax.rem(shift, RING)
    k = lax.div(shift, RING)
    out_ref[WAY] = k * (KEY_HOPS + 1) + jnp.minimum(h, KEY_HOPS) - 1
    out_ref[AROUND] = jnp.maximum(h, KEY_HOPS - 1) - (KEY_HOPS - 1)
    out_ref[COL] = m
    out_ref[COL + 1] = 0

    def wrapped(i):
        return lax.rem(i + 2 * owners, owners)

    for n in range(2):
        col = m if n == 0 else 1 - m
        sign = 1 - 2 * n
        hops = jnp.minimum(h + n, KEY_HOPS)
        out_ref[DEC_LEN + n] = dec_ref[n, own]
        out_ref[ENC_LEN + n] = enc_ref[n, own]
        out_ref[KEY_LEN + n] = enc_ref[col, wrapped(own - sign * (RING * k + hops))]
        out_ref[QUERY_LEN + n] = dec_ref[col, wrapped(own + sign * (h + n - hops))]
    for n in range(QUERY_LEN + 2, out_ref.shape[0]):
        out_ref[n] = 0
    for copy in copies:
        copy.wait()
    cap, total = kvm_ref.shape[1], k_ref.shape[0]
    pick = one_hot((cap, total), enc_ref[0, own])
    for c, ref in enumerate((k_ref, v_ref)):
        first = ref[:cap]
        second = dot(pick, ref[...]).astype(first.dtype)
        kvm_ref[c] = jnp.where(m == 0, first, second)
        kvn_ref[c] = jnp.where(m == 0, second, first)


def prepare(own, enc, dec, target, keys, values, owners, cap):
    slot = jax.ShapeDtypeStruct((2, cap, HEAD_DIM), keys.dtype)
    return pl.pallas_call(
        functools.partial(prepare_kernel, owners),
        in_specs=[SMEM] * 4 + [pl.BlockSpec(memory_space=pl.ANY)] * 2,
        out_specs=[SMEM] + [pl.BlockSpec()] * 2,
        out_shape=[jax.ShapeDtypeStruct((16,), jnp.int32), slot, slot],
        scratch_shapes=[pltpu.VMEM(keys.shape, keys.dtype)] * 2 + [pltpu.SemaphoreType.DMA((2,))],
        compiler_params=WIDE,
    )(own, enc, dec, target, keys, values)


def split_kernel(q_ref, g_ref, parts_ref):
    for j in range(parts_ref.shape[0]):
        for c, in_ref in enumerate((q_ref, g_ref)):
            parts_ref[j, c] = in_ref[:, j * HEAD_DIM : (j + 1) * HEAD_DIM]


def split(queries, grads):
    rows, width = queries.shape
    return pl.pallas_call(
        split_kernel,
        out_shape=jax.ShapeDtypeStruct((width // HEAD_DIM, 2, rows, HEAD_DIM), queries.dtype),
        compiler_params=PARAMS,
    )(queries, grads)


def join_kernel(parts_ref, *outs):
    for j in range(parts_ref.shape[0]):
        for c, out_ref in enumerate(outs):
            out_ref[:, j * HEAD_DIM : (j + 1) * HEAD_DIM] = parts_ref[j, c]


def join(parts):
    heads, count, rows, _ = parts.shape
    return pl.pallas_call(
        join_kernel,
        out_shape=[jax.ShapeDtypeStruct((rows, heads * HEAD_DIM), parts.dtype)] * count,
        compiler_params=PARAMS,
    )(parts)


def pack_kernel(scal, in_ref, xm_ref, xn_ref):
    size, count, rows, _ = in_ref.shape
    m, len0, len1 = scal[COL], scal[DEC_LEN], scal[DEC_LEN + 1]

    def part(j, _):
        base = pl.multiple_of(j * rows, rows)
        at = pl.ds(base, rows)
        pick = one_hot((rows, size * rows), len0 + base)
        at_row = lax.broadcasted_iota(jnp.int32, (rows, 1), 0) + base
        for c in range(count):
            first = in_ref[j, c]
            first = jnp.where(at_row < len0, first, jnp.zeros_like(first))
            second = dot(pick, in_ref[:, c].reshape(size * rows, HEAD_DIM))
            second = jnp.where(at_row < len1, second, 0.0).astype(first.dtype)
            xm_ref[c, at, :] = jnp.where(m == 0, first, second)
            xn_ref[c, at, :] = jnp.where(m == 0, second, first)
        return 0

    lax.fori_loop(0, xm_ref.shape[1] // rows, part, 0)


def pack(scal, parts, cap):
    slot = jax.ShapeDtypeStruct((parts.shape[1], cap, HEAD_DIM), parts.dtype)
    return pl.pallas_call(
        pack_kernel,
        in_specs=[SMEM, pl.BlockSpec()],
        out_shape=[slot, slot],
        compiler_params=PARAMS,
    )(scal, parts)


def merge_parts_kernel(scal, a_ref, b_ref, parts_ref):
    size, count, rows, _ = parts_ref.shape
    cap = a_ref.shape[1]
    m, len0 = scal[COL], scal[DEC_LEN]

    def part(j, _):
        base = j * rows
        at = pl.ds(pl.multiple_of(jnp.minimum(base, cap - rows), rows), rows)
        pick = one_hot((rows, cap), base - len0)
        for c in range(count):
            first = jnp.where(m == 0, a_ref[c, at, :], b_ref[c, at, :])
            second = jnp.where(m == 0, b_ref[c], a_ref[c])
            first = jnp.where(base < cap, first, jnp.zeros_like(first)).astype(jnp.float32)
            parts_ref[j, c] = (dot(pick, second) + first).astype(parts_ref.dtype)
        return 0

    lax.fori_loop(0, size, part, 0)


def merge_parts(scal, a, b, parts):
    rows = a.shape[1] * 2 // parts
    return pl.pallas_call(
        merge_parts_kernel,
        in_specs=[SMEM, pl.BlockSpec(), pl.BlockSpec()],
        out_shape=jax.ShapeDtypeStruct((parts, a.shape[0], rows, HEAD_DIM), a.dtype),
        compiler_params=PARAMS,
    )(scal, a, b)


def merge_keys_kernel(scal, a_ref, b_ref, *outs):
    cap, total = a_ref.shape[1], outs[0].shape[0]
    m, len0 = scal[COL], scal[ENC_LEN]
    low = cap // 2
    pick = one_hot((total - low, cap), low - len0)
    for c, out_ref in enumerate(outs):
        first = jnp.where(m == 0, a_ref[c], b_ref[c])
        second = jnp.where(m == 0, b_ref[c], a_ref[c])
        moved = dot(pick, second)
        out_ref[:low] = first[:low]
        out_ref[low:cap] = (moved[: cap - low] + first[low:].astype(jnp.float32)).astype(out_ref.dtype)
        out_ref[cap:] = moved[cap - low :].astype(out_ref.dtype)


def merge_keys(scal, a, b, total):
    return pl.pallas_call(
        merge_keys_kernel,
        in_specs=[SMEM, pl.BlockSpec(), pl.BlockSpec()],
        out_shape=[jax.ShapeDtypeStruct((total, HEAD_DIM), a.dtype)] * a.shape[0],
        compiler_params=PARAMS,
    )(scal, a, b)


def attend_rows(q, g, keys, values, key_len, valid):
    scores = dot(q, keys, NT) * SCALING
    col = lax.broadcasted_iota(jnp.int32, (1, scores.shape[1]), 1)
    scores = jnp.where(col < key_len, scores, -1e30)
    raised = jnp.exp(scores - jnp.max(scores, axis=1, keepdims=True))
    probs = raised * (1.0 / jnp.sum(raised, axis=1, keepdims=True))
    probs_b = probs.astype(jnp.bfloat16)
    prob_grad = dot(g, values, NT)
    row_dot = jnp.sum(probs * prob_grad, axis=1, keepdims=True)
    score_grad = (probs * (prob_grad - row_dot)).astype(jnp.bfloat16)
    context = jnp.where(valid, dot(probs_b, values), 0.0).astype(jnp.bfloat16)
    query_grad = jnp.where(valid, dot(score_grad, keys) * SCALING, 0.0).astype(jnp.bfloat16)
    return context, query_grad, probs_b, score_grad


def attend_kernel(scal, xm_ref, xn_ref, kvm_ref, kvn_ref, ym_ref, yn_ref, dkvm_ref, dkvn_ref):
    columns = ((xm_ref, kvm_ref, ym_ref, dkvm_ref), (xn_ref, kvn_ref, yn_ref, dkvn_ref))
    for n, (x_ref, kv_ref, y_ref, dkv_ref) in enumerate(columns):
        probs, score_grads = [], []
        for base in range(0, x_ref.shape[1], ROWS):
            at = slice(base, base + ROWS)
            valid = lax.broadcasted_iota(jnp.int32, (ROWS, 1), 0) + base < scal[QUERY_LEN + n]
            y_ref[0, at], y_ref[1, at], probs_b, score_grad = attend_rows(
                x_ref[0, at], x_ref[1, at], kv_ref[0], kv_ref[1], scal[KEY_LEN + n], valid
            )
            probs.append(probs_b)
            score_grads.append(score_grad)
        key_grad = dot(jnp.concatenate(score_grads), x_ref[0], TN) * SCALING
        dkv_ref[0] = key_grad.astype(dkv_ref.dtype)
        dkv_ref[1] = dot(jnp.concatenate(probs), x_ref[1], TN).astype(dkv_ref.dtype)


def attend(scal, xm, xn, kvm, kvn):
    cap, keys = xm.shape[1], kvm.shape[1]
    return pl.pallas_call(
        attend_kernel,
        in_specs=[SMEM] + [pl.BlockSpec()] * 4,
        out_shape=[jax.ShapeDtypeStruct(a.shape, a.dtype) for a in (xm, xn, kvm, kvn)],
        compiler_params=PARAMS,
        cost_estimate=pl.CostEstimate(
            flops=24 * cap * keys * HEAD_DIM, bytes_accessed=5 * 2**20, transcendentals=2 * cap * keys
        ),
    )(scal, xm, xn, kvm, kvn)


def exchanged(parts, flag):
    def swap(parts):
        return lax.all_to_all(parts, "mp", split_axis=0, concat_axis=0, tiled=True)

    return lax.cond(flag, swap, lambda parts: parts, parts)


def local(
    queries,
    encoder_keys,
    encoder_values,
    context_grad,
    encoder_lengths,
    decoder_lengths,
    target_device,
):
    owners = lax.axis_size("dp")
    own = lax.axis_index("dp").astype(jnp.int32).reshape(1)
    seq_count = target_device.shape[1]
    dec_total = queries.shape[0] * lax.axis_size("mp")
    dec_cap = dec_total // seq_count
    enc_total = encoder_keys.shape[0]
    enc_cap = enc_total // seq_count
    scal, kvm, kvn = prepare(
        own, encoder_lengths.T, decoder_lengths.T, target_device.T, encoder_keys, encoder_values, owners, enc_cap
    )
    way, around = scal[WAY], scal[AROUND]
    ways = [
        (RING * i + min(j, KEY_HOPS), RING * i + min(j + 1, KEY_HOPS))
        for i in range(owners // RING)
        for j in range(KEY_HOPS + 1)
    ][1:]
    rest = [(max(j - KEY_HOPS, 0), j + 1 - KEY_HOPS) for j in range(KEY_HOPS - 1, RING // 2)]

    def queries_out(m, n):
        def run(xm, xn):
            xn = queries_along(xn, n)
            return xn, queries_along(xm, -m)

        return run

    def out_along(m, n, last):
        def run(scal, around, kvm, kvn, queries, context_grad):
            kvn = passed_along(kvn, -n)
            kvm = passed_along(kvm, m)
            xm, xn = pack(scal, exchanged(split(queries, context_grad), around >= 0), dec_cap)
            if last:
                xn, xm = lax.switch(around - 1, [queries_out(*r) for r in rest[1:]], xm, xn)
            return kvn, kvm, xn, xm

        return run

    kvn, kvm, xn, xm = lax.switch(
        way,
        [out_along(*w, i % (KEY_HOPS + 1) == KEY_HOPS - 1) for i, w in enumerate(ways)],
        scal, around, kvm, kvn, queries, context_grad,
    )

    def queries_back(m, n):
        def run(ym, yn):
            yn = queries_along(yn, -n)
            return yn, queries_along(ym, m)

        return run

    ym, yn, kvm, kvn = attend(scal, xm, xn, kvm, kvn)
    yn, ym = lax.switch(around, [queries_back(*r) for r in rest], ym, yn)

    def back_along(m, n):
        def run(scal, around, kvm, kvn, ym, yn):
            kvn = passed_along(kvn, n)
            kvm = passed_along(kvm, -m)
            parts = merge_parts(scal, ym, yn, lax.axis_size("mp"))
            return kvn, kvm, *join(exchanged(parts, around >= 0))

        return run

    kvn, kvm, context, query_grad = lax.switch(
        way, [back_along(*w) for w in ways], scal, around, kvm, kvn, ym, yn
    )
    key_grad, value_grad = merge_keys(scal, kvm, kvn, enc_total)
    return (context, query_grad, key_grad, value_grad)


def solution(mesh):
    return jax.shard_map(
        local,
        mesh=mesh,
        in_specs=(
            P(("dp", "mp"), None),
            P("dp", "mp"),
            P("dp", "mp"),
            P(("dp", "mp"), None),
            P(),
            P(),
            P(),
        ),
        out_specs=(P(("dp", "mp"), None), P(("dp", "mp"), None), P("dp", "mp"), P("dp", "mp")),
        check_vma=False,
    )
```

```python
import functools

import jax
import jax.numpy as jnp
from jax import lax
from jax.experimental import pallas as pl
from jax.experimental.pallas import tpu as pltpu
from jax.sharding import PartitionSpec as P

HEAD_DIM = 256
SCALING = HEAD_DIM ** (-0.5)
ROWS = 256
RING = 16
KEY_HOPS = ((0, 1), (1, 2), (2, 3), (2, 2))
SMEM = pl.BlockSpec(memory_space=pltpu.SMEM)
NT = (((1,), (1,)), ((), ()))
TN = (((0,), (0,)), ((), ()))
COL, DEC_LEN, ENC_LEN, KEY_LEN, QUERY_LEN = 0, 2, 4, 6, 8
PARAMS = pltpu.CompilerParams(vmem_limit_bytes=32 * 2**20)
WIDE = pltpu.CompilerParams(vmem_limit_bytes=60 * 2**20)


def dot(a, b, dims=(((1,), (0,)), ((), ()))):
    return lax.dot_general(a, b, dims, preferred_element_type=jnp.float32)


def passed_along(block, distance):
    owners = lax.axis_size("dp")
    if distance % owners == 0:
        return block
    return lax.ppermute(block, "dp", [(i, (i + distance) % owners) for i in range(owners)])


def copy_kernel(in_ref, out_ref):
    out_ref[...] = in_ref[...]


def queries_along(block, distance):
    if distance:
        return passed_along(block, distance)
    return pl.pallas_call(
        copy_kernel,
        out_shape=jax.ShapeDtypeStruct(block.shape, block.dtype),
        compiler_params=PARAMS,
    )(block)


def one_hot(shape, gap):
    row = lax.broadcasted_iota(jnp.int32, shape, 0)
    col = lax.broadcasted_iota(jnp.int32, shape, 1)
    return (col - row == gap).astype(jnp.float32).astype(jnp.bfloat16)


def prepare_kernel(
    owners, own_ref, enc_ref, dec_ref, target_ref, k_hbm, v_hbm, way_ref, around_ref, out_ref, kvm_ref, kvn_ref, k_ref, v_ref, sems
):
    copies = [
        pltpu.make_async_copy(k_hbm, k_ref, sems.at[0]),
        pltpu.make_async_copy(v_hbm, v_ref, sems.at[1]),
    ]
    for copy in copies:
        copy.start()
    own = own_ref[0]
    shift0 = lax.rem(target_ref[0, 0], owners)
    m = jnp.where(lax.rem(shift0, RING) < RING // 2, 0, 1)
    shift = jnp.where(m == 0, shift0, owners - 1 - shift0)
    h = lax.rem(shift, RING)
    k = lax.div(shift, RING)
    way_ref[0] = k * len(KEY_HOPS) + jnp.minimum(h, len(KEY_HOPS) - 1) - 1
    around_ref[0] = jnp.maximum(h, len(KEY_HOPS) - 2) - (len(KEY_HOPS) - 2)
    out_ref[COL] = m
    out_ref[COL + 1] = 0

    def wrapped(i):
        return lax.rem(i + 2 * owners, owners)

    for n in range(2):
        col = m if n == 0 else 1 - m
        sign = 1 - 2 * n
        hops = KEY_HOPS[-1][n]
        for j in range(len(KEY_HOPS) - 1):
            hops = jnp.where(h == j, KEY_HOPS[j][n], hops)
        out_ref[DEC_LEN + n] = dec_ref[n, own]
        out_ref[ENC_LEN + n] = enc_ref[n, own]
        out_ref[KEY_LEN + n] = enc_ref[col, wrapped(own - sign * (RING * k + hops))]
        out_ref[QUERY_LEN + n] = dec_ref[col, wrapped(own + sign * (h + n - hops))]
    for n in range(QUERY_LEN + 2, out_ref.shape[0]):
        out_ref[n] = 0
    for copy in copies:
        copy.wait()
    cap, total = kvm_ref.shape[1], k_ref.shape[0]
    pick = one_hot((cap, total), enc_ref[0, own])
    for c, ref in enumerate((k_ref, v_ref)):
        first = ref[:cap]
        second = dot(pick, ref[...]).astype(first.dtype)
        kvm_ref[c] = jnp.where(m == 0, first, second)
        kvn_ref[c] = jnp.where(m == 0, second, first)


def prepare(own, enc, dec, target, keys, values, owners, cap):
    slot = jax.ShapeDtypeStruct((2, cap, HEAD_DIM), keys.dtype)
    return pl.pallas_call(
        functools.partial(prepare_kernel, owners),
        in_specs=[SMEM] * 4 + [pl.BlockSpec(memory_space=pl.ANY)] * 2,
        out_specs=[SMEM] * 3 + [pl.BlockSpec()] * 2,
        out_shape=[jax.ShapeDtypeStruct((size,), jnp.int32) for size in (1, 1, 16)] + [slot, slot],
        scratch_shapes=[pltpu.VMEM(keys.shape, keys.dtype)] * 2 + [pltpu.SemaphoreType.DMA((2,))],
        compiler_params=WIDE,
    )(own, enc, dec, target, keys, values)


def split_kernel(q_ref, g_ref, parts_ref):
    for j in range(parts_ref.shape[0]):
        for c, in_ref in enumerate((q_ref, g_ref)):
            parts_ref[j, c] = in_ref[:, j * HEAD_DIM : (j + 1) * HEAD_DIM]


def split(queries, grads):
    rows, width = queries.shape
    return pl.pallas_call(
        split_kernel,
        out_shape=jax.ShapeDtypeStruct((width // HEAD_DIM, 2, rows, HEAD_DIM), queries.dtype),
        compiler_params=PARAMS,
    )(queries, grads)


def join_kernel(parts_ref, *outs):
    for j in range(parts_ref.shape[0]):
        for c, out_ref in enumerate(outs):
            out_ref[:, j * HEAD_DIM : (j + 1) * HEAD_DIM] = parts_ref[j, c]


def join(parts):
    heads, count, rows, _ = parts.shape
    return pl.pallas_call(
        join_kernel,
        out_shape=[jax.ShapeDtypeStruct((rows, heads * HEAD_DIM), parts.dtype)] * count,
        compiler_params=PARAMS,
    )(parts)


def pack_kernel(scal, in_ref, xm_ref, xn_ref):
    size, count, rows, _ = in_ref.shape
    m, len0, len1 = scal[COL], scal[DEC_LEN], scal[DEC_LEN + 1]

    def part(j, _):
        base = pl.multiple_of(j * rows, rows)
        at = pl.ds(base, rows)
        pick = one_hot((rows, size * rows), len0 + base)
        at_row = lax.broadcasted_iota(jnp.int32, (rows, 1), 0) + base
        for c in range(count):
            first = in_ref[j, c]
            first = jnp.where(at_row < len0, first, jnp.zeros_like(first))
            second = dot(pick, in_ref[:, c].reshape(size * rows, HEAD_DIM))
            second = jnp.where(at_row < len1, second, 0.0).astype(first.dtype)
            xm_ref[c, at, :] = jnp.where(m == 0, first, second)
            xn_ref[c, at, :] = jnp.where(m == 0, second, first)
        return 0

    lax.fori_loop(0, xm_ref.shape[1] // rows, part, 0)


def pack(scal, parts, cap):
    slot = jax.ShapeDtypeStruct((parts.shape[1], cap, HEAD_DIM), parts.dtype)
    return pl.pallas_call(
        pack_kernel,
        in_specs=[SMEM, pl.BlockSpec()],
        out_shape=[slot, slot],
        compiler_params=PARAMS,
    )(scal, parts)


def merge_parts_kernel(scal, a_ref, b_ref, parts_ref):
    size, count, rows, _ = parts_ref.shape
    cap = a_ref.shape[1]
    m, len0 = scal[COL], scal[DEC_LEN]

    def part(j, _):
        base = j * rows
        at = pl.ds(pl.multiple_of(jnp.minimum(base, cap - rows), rows), rows)
        pick = one_hot((rows, cap), base - len0)
        for c in range(count):
            first = jnp.where(m == 0, a_ref[c, at, :], b_ref[c, at, :])
            second = jnp.where(m == 0, b_ref[c], a_ref[c])
            first = jnp.where(base < cap, first, jnp.zeros_like(first)).astype(jnp.float32)
            parts_ref[j, c] = (dot(pick, second) + first).astype(parts_ref.dtype)
        return 0

    lax.fori_loop(0, size, part, 0)


def merge_parts(scal, a, b, parts):
    rows = a.shape[1] * 2 // parts
    return pl.pallas_call(
        merge_parts_kernel,
        in_specs=[SMEM, pl.BlockSpec(), pl.BlockSpec()],
        out_shape=jax.ShapeDtypeStruct((parts, a.shape[0], rows, HEAD_DIM), a.dtype),
        compiler_params=PARAMS,
    )(scal, a, b)


def merge_keys_kernel(scal, a_ref, b_ref, *outs):
    cap, total = a_ref.shape[1], outs[0].shape[0]
    m, len0 = scal[COL], scal[ENC_LEN]
    low = cap // 2
    pick = one_hot((total - low, cap), low - len0)
    for c, out_ref in enumerate(outs):
        first = jnp.where(m == 0, a_ref[c], b_ref[c])
        second = jnp.where(m == 0, b_ref[c], a_ref[c])
        moved = dot(pick, second)
        out_ref[:low] = first[:low]
        out_ref[low:cap] = (moved[: cap - low] + first[low:].astype(jnp.float32)).astype(out_ref.dtype)
        out_ref[cap:] = moved[cap - low :].astype(out_ref.dtype)


def merge_keys(scal, a, b, total):
    return pl.pallas_call(
        merge_keys_kernel,
        in_specs=[SMEM, pl.BlockSpec(), pl.BlockSpec()],
        out_shape=[jax.ShapeDtypeStruct((total, HEAD_DIM), a.dtype)] * a.shape[0],
        compiler_params=PARAMS,
    )(scal, a, b)


def attend_rows(q, g, keys, values, key_len, valid):
    scores = dot(q, keys, NT) * SCALING
    col = lax.broadcasted_iota(jnp.int32, (1, scores.shape[1]), 1)
    scores = jnp.where(col < key_len, scores, -1e30)
    raised = jnp.exp(scores - jnp.max(scores, axis=1, keepdims=True))
    probs = raised * (1.0 / jnp.sum(raised, axis=1, keepdims=True))
    probs_b = probs.astype(jnp.bfloat16)
    prob_grad = dot(g, values, NT)
    row_dot = jnp.sum(probs * prob_grad, axis=1, keepdims=True)
    score_grad = (probs * (prob_grad - row_dot)).astype(jnp.bfloat16)
    context = jnp.where(valid, dot(probs_b, values), 0.0).astype(jnp.bfloat16)
    query_grad = jnp.where(valid, dot(score_grad, keys) * SCALING, 0.0).astype(jnp.bfloat16)
    return context, query_grad, probs_b, score_grad


def attend_kernel(n, scal, x_ref, kv_ref, y_ref, dkv_ref):
    probs, score_grads = [], []
    for base in range(0, x_ref.shape[1], ROWS):
        at = slice(base, base + ROWS)
        valid = lax.broadcasted_iota(jnp.int32, (ROWS, 1), 0) + base < scal[QUERY_LEN + n]
        y_ref[0, at], y_ref[1, at], probs_b, score_grad = attend_rows(
            x_ref[0, at], x_ref[1, at], kv_ref[0], kv_ref[1], scal[KEY_LEN + n], valid
        )
        probs.append(probs_b)
        score_grads.append(score_grad)
    key_grad = dot(jnp.concatenate(score_grads), x_ref[0], TN) * SCALING
    dkv_ref[0] = key_grad.astype(dkv_ref.dtype)
    dkv_ref[1] = dot(jnp.concatenate(probs), x_ref[1], TN).astype(dkv_ref.dtype)


def attend_small_kernel(n, scal, x_ref, kv_ref, y_ref, dkv_ref, acc_ref):
    step = pl.program_id(0)
    rows = x_ref.shape[1]
    valid = lax.broadcasted_iota(jnp.int32, (rows, 1), 0) + step * rows < scal[QUERY_LEN + n]
    y_ref[0], y_ref[1], probs_b, score_grad = attend_rows(
        x_ref[0], x_ref[1], kv_ref[0], kv_ref[1], scal[KEY_LEN + n], valid
    )

    @pl.when(step == 0)
    def _():
        acc_ref[...] = jnp.zeros_like(acc_ref)

    acc_ref[0] += dot(score_grad, x_ref[0], TN)
    acc_ref[1] += dot(probs_b, x_ref[1], TN)

    @pl.when(step == pl.num_programs(0) - 1)
    def _():
        dkv_ref[0] = (acc_ref[0] * SCALING).astype(dkv_ref.dtype)
        dkv_ref[1] = acc_ref[1].astype(dkv_ref.dtype)


def attend(n, scal, x, kv, small):
    cap, keys = x.shape[1], kv.shape[1]
    if small:
        blocks = pl.BlockSpec((2, ROWS // 2, HEAD_DIM), lambda i: (0, i, 0))
        whole = pl.BlockSpec(kv.shape, lambda i: (0, 0, 0))
        how = dict(
            grid=(cap // (ROWS // 2),),
            in_specs=[SMEM, blocks, whole],
            out_specs=[blocks, whole],
            scratch_shapes=[pltpu.VMEM(kv.shape, jnp.float32)],
        )
    else:
        how = dict(in_specs=[SMEM, pl.BlockSpec(), pl.BlockSpec()])
    return pl.pallas_call(
        functools.partial(attend_small_kernel if small else attend_kernel, n),
        out_shape=[jax.ShapeDtypeStruct(a.shape, a.dtype) for a in (x, kv)],
        compiler_params=PARAMS,
        cost_estimate=pl.CostEstimate(
            flops=12 * cap * keys * HEAD_DIM, bytes_accessed=3 * 2**20, transcendentals=cap * keys
        ),
        **how,
    )(scal, x, kv)


def exchanged(parts, flag):
    def swap(parts):
        return lax.all_to_all(parts, "mp", split_axis=0, concat_axis=0, tiled=True)

    return lax.cond(flag, swap, lambda parts: parts, parts)


def local(
    queries,
    encoder_keys,
    encoder_values,
    context_grad,
    encoder_lengths,
    decoder_lengths,
    target_device,
):
    owners = lax.axis_size("dp")
    own = lax.axis_index("dp").astype(jnp.int32).reshape(1)
    seq_count = target_device.shape[1]
    dec_total = queries.shape[0] * lax.axis_size("mp")
    dec_cap = dec_total // seq_count
    enc_total = encoder_keys.shape[0]
    enc_cap = enc_total // seq_count
    way, around, scal, kvm, kvn = prepare(
        own, encoder_lengths.T, decoder_lengths.T, target_device.T, encoder_keys, encoder_values, owners, enc_cap
    )
    way, around = way[0], around[0]
    ways = [(RING * i + m, RING * i + n) for i in range(owners // RING) for m, n in KEY_HOPS][1:]
    last = len(KEY_HOPS) - 1
    rest = [(0, 0)] + [(j - KEY_HOPS[-1][0], j + 1 - KEY_HOPS[-1][1]) for j in range(last, RING // 2)]

    def queries_out(m, n):
        def run(xm, xn):
            xn = passed_along(xn, n)
            return xn, passed_along(xm, -m)

        return run

    def out_along(m, n, last):
        def run(scal, around, kvm, kvn, queries, context_grad):
            kvn = passed_along(kvn, -n)
            kvm = passed_along(kvm, m)
            xm, xn = pack(scal, exchanged(split(queries, context_grad), around >= 0), dec_cap)
            if last:
                xn, xm = lax.switch(around - 1, [queries_out(*r) for r in rest[1:]], xm, xn)
            return kvn, kvm, xn, xm

        return run

    kvn, kvm, xn, xm = lax.switch(
        way,
        [out_along(*w, i % len(KEY_HOPS) == last - 1) for i, w in enumerate(ways)],
        scal, around, kvm, kvn, queries, context_grad,
    )

    def queries_back(m, n):
        def run(scal, yn, xm, kvm):
            yn = queries_along(yn, -n)
            ym, kvm = attend(0, scal, xm, kvm, m > 0)
            return yn, passed_along(ym, m), kvm

        return run

    yn, kvn = attend(1, scal, xn, kvn, False)
    yn, ym, kvm = lax.switch(around, [queries_back(*r) for r in rest], scal, yn, xm, kvm)

    def back_along(m, n):
        def run(scal, around, kvm, kvn, ym, yn):
            kvn = passed_along(kvn, n)
            kvm = passed_along(kvm, -m)
            parts = merge_parts(scal, ym, yn, lax.axis_size("mp"))
            return kvn, kvm, *join(exchanged(parts, around >= 0))

        return run

    kvn, kvm, context, query_grad = lax.switch(
        way, [back_along(*w) for w in ways], scal, around, kvm, kvn, ym, yn
    )
    key_grad, value_grad = merge_keys(scal, kvm, kvn, enc_total)
    return (context, query_grad, key_grad, value_grad)


def solution(mesh):
    return jax.shard_map(
        local,
        mesh=mesh,
        in_specs=(
            P(("dp", "mp"), None),
            P("dp", "mp"),
            P("dp", "mp"),
            P(("dp", "mp"), None),
            P(),
            P(),
            P(),
        ),
        out_specs=(P(("dp", "mp"), None), P(("dp", "mp"), None), P("dp", "mp"), P("dp", "mp")),
        check_vma=False,
    )
```

```python
import functools

import jax
import jax.numpy as jnp
from jax import lax
from jax.experimental import pallas as pl
from jax.experimental.pallas import tpu as pltpu
from jax.sharding import PartitionSpec as P

HEAD_DIM = 256
SCALING = HEAD_DIM ** (-0.5)
ROWS = 256
RING = 16
KEY_HOPS = ((0, 1), (1, 2), (2, 3), (2, 2))
SMEM = pl.BlockSpec(memory_space=pltpu.SMEM)
NT = (((1,), (1,)), ((), ()))
TN = (((0,), (0,)), ((), ()))
COL, DEC_LEN, ENC_LEN, KEY_LEN, QUERY_LEN = 0, 2, 4, 6, 8
PARAMS = pltpu.CompilerParams(vmem_limit_bytes=32 * 2**20)
WIDE = pltpu.CompilerParams(vmem_limit_bytes=60 * 2**20)


def dot(a, b, dims=(((1,), (0,)), ((), ()))):
    return lax.dot_general(a, b, dims, preferred_element_type=jnp.float32)


def passed_along(block, distance):
    owners = lax.axis_size("dp")
    if distance % owners == 0:
        return block
    return lax.ppermute(block, "dp", [(i, (i + distance) % owners) for i in range(owners)])


def copy_kernel(in_ref, out_ref):
    out_ref[...] = in_ref[...]


def queries_along(block, distance):
    if distance:
        return passed_along(block, distance)
    return pl.pallas_call(
        copy_kernel,
        out_shape=jax.ShapeDtypeStruct(block.shape, block.dtype),
        compiler_params=PARAMS,
    )(block)


def one_hot(shape, gap):
    row = lax.broadcasted_iota(jnp.int32, shape, 0)
    col = lax.broadcasted_iota(jnp.int32, shape, 1)
    return (col - row == gap).astype(jnp.float32).astype(jnp.bfloat16)


def prepare_kernel(
    owners, own_ref, enc_ref, dec_ref, target_ref, k_hbm, v_hbm, way_ref, around_ref, out_ref, kvm_ref, kvn_ref, k_ref, v_ref, sems
):
    copies = [
        pltpu.make_async_copy(k_hbm, k_ref, sems.at[0]),
        pltpu.make_async_copy(v_hbm, v_ref, sems.at[1]),
    ]
    for copy in copies:
        copy.start()
    own = own_ref[0]
    shift0 = lax.rem(target_ref[0, 0], owners)
    m = jnp.where(lax.rem(shift0, RING) < RING // 2, 0, 1)
    shift = jnp.where(m == 0, shift0, owners - 1 - shift0)
    h = lax.rem(shift, RING)
    k = lax.div(shift, RING)
    way_ref[0] = k * len(KEY_HOPS) + jnp.minimum(h, len(KEY_HOPS) - 1) - 1
    around_ref[0] = jnp.maximum(h, len(KEY_HOPS) - 2) - (len(KEY_HOPS) - 2)
    out_ref[COL] = m
    out_ref[COL + 1] = 0

    def wrapped(i):
        return lax.rem(i + 2 * owners, owners)

    for n in range(2):
        col = m if n == 0 else 1 - m
        sign = 1 - 2 * n
        hops = KEY_HOPS[-1][n]
        for j in range(len(KEY_HOPS) - 1):
            hops = jnp.where(h == j, KEY_HOPS[j][n], hops)
        out_ref[DEC_LEN + n] = dec_ref[n, own]
        out_ref[ENC_LEN + n] = enc_ref[n, own]
        out_ref[KEY_LEN + n] = enc_ref[col, wrapped(own - sign * (RING * k + hops))]
        out_ref[QUERY_LEN + n] = dec_ref[col, wrapped(own + sign * (h + n - hops))]
    for n in range(QUERY_LEN + 2, out_ref.shape[0]):
        out_ref[n] = 0
    for copy in copies:
        copy.wait()
    cap, total = kvm_ref.shape[1], k_ref.shape[0]
    pick = one_hot((cap, total), enc_ref[0, own])
    for c, ref in enumerate((k_ref, v_ref)):
        first = ref[:cap]
        second = dot(pick, ref[...]).astype(first.dtype)
        kvm_ref[c] = jnp.where(m == 0, first, second)
        kvn_ref[c] = jnp.where(m == 0, second, first)


def prepare(own, enc, dec, target, keys, values, owners, cap):
    slot = jax.ShapeDtypeStruct((2, cap, HEAD_DIM), keys.dtype)
    return pl.pallas_call(
        functools.partial(prepare_kernel, owners),
        in_specs=[SMEM] * 4 + [pl.BlockSpec(memory_space=pl.ANY)] * 2,
        out_specs=[SMEM] * 3 + [pl.BlockSpec()] * 2,
        out_shape=[jax.ShapeDtypeStruct((size,), jnp.int32) for size in (1, 1, 16)] + [slot, slot],
        scratch_shapes=[pltpu.VMEM(keys.shape, keys.dtype)] * 2 + [pltpu.SemaphoreType.DMA((2,))],
        compiler_params=WIDE,
    )(own, enc, dec, target, keys, values)


def split_kernel(q_ref, g_ref, parts_ref):
    for j in range(parts_ref.shape[0]):
        for c, in_ref in enumerate((q_ref, g_ref)):
            parts_ref[j, c] = in_ref[:, j * HEAD_DIM : (j + 1) * HEAD_DIM]


def split(queries, grads):
    rows, width = queries.shape
    return pl.pallas_call(
        split_kernel,
        out_shape=jax.ShapeDtypeStruct((width // HEAD_DIM, 2, rows, HEAD_DIM), queries.dtype),
        compiler_params=PARAMS,
    )(queries, grads)


def join_kernel(parts_ref, *outs):
    for j in range(parts_ref.shape[0]):
        for c, out_ref in enumerate(outs):
            out_ref[:, j * HEAD_DIM : (j + 1) * HEAD_DIM] = parts_ref[j, c]


def join(parts):
    heads, count, rows, _ = parts.shape
    return pl.pallas_call(
        join_kernel,
        out_shape=[jax.ShapeDtypeStruct((rows, heads * HEAD_DIM), parts.dtype)] * count,
        compiler_params=PARAMS,
    )(parts)


def pack_kernel(scal, in_ref, xm_ref, xn_ref):
    size, count, rows, _ = in_ref.shape
    m, len0, len1 = scal[COL], scal[DEC_LEN], scal[DEC_LEN + 1]

    def part(j, _):
        base = pl.multiple_of(j * rows, rows)
        at = pl.ds(base, rows)
        pick = one_hot((rows, size * rows), len0 + base)
        at_row = lax.broadcasted_iota(jnp.int32, (rows, 1), 0) + base
        for c in range(count):
            first = in_ref[j, c]
            first = jnp.where(at_row < len0, first, jnp.zeros_like(first))
            second = dot(pick, in_ref[:, c].reshape(size * rows, HEAD_DIM))
            second = jnp.where(at_row < len1, second, 0.0).astype(first.dtype)
            xm_ref[c, at, :] = jnp.where(m == 0, first, second)
            xn_ref[c, at, :] = jnp.where(m == 0, second, first)
        return 0

    lax.fori_loop(0, xm_ref.shape[1] // rows, part, 0)


def pack(scal, parts, cap):
    slot = jax.ShapeDtypeStruct((parts.shape[1], cap, HEAD_DIM), parts.dtype)
    return pl.pallas_call(
        pack_kernel,
        in_specs=[SMEM, pl.BlockSpec()],
        out_shape=[slot, slot],
        compiler_params=PARAMS,
    )(scal, parts)


def merge_parts_kernel(scal, a_ref, b_ref, parts_ref):
    size, count, rows, _ = parts_ref.shape
    cap = a_ref.shape[1]
    m, len0 = scal[COL], scal[DEC_LEN]

    def part(j, _):
        base = j * rows
        at = pl.ds(pl.multiple_of(jnp.minimum(base, cap - rows), rows), rows)
        pick = one_hot((rows, cap), base - len0)
        for c in range(count):
            first = jnp.where(m == 0, a_ref[c, at, :], b_ref[c, at, :])
            second = jnp.where(m == 0, b_ref[c], a_ref[c])
            first = jnp.where(base < cap, first, jnp.zeros_like(first)).astype(jnp.float32)
            parts_ref[j, c] = (dot(pick, second) + first).astype(parts_ref.dtype)
        return 0

    lax.fori_loop(0, size, part, 0, unroll=2)


def merge_parts(scal, a, b, parts):
    rows = a.shape[1] * 2 // parts
    return pl.pallas_call(
        merge_parts_kernel,
        in_specs=[SMEM, pl.BlockSpec(), pl.BlockSpec()],
        out_shape=jax.ShapeDtypeStruct((parts, a.shape[0], rows, HEAD_DIM), a.dtype),
        compiler_params=PARAMS,
    )(scal, a, b)


def merge_keys_kernel(scal, a_ref, b_ref, *outs):
    cap, total = a_ref.shape[1], outs[0].shape[0]
    m, len0 = scal[COL], scal[ENC_LEN]
    low = cap // 2
    pick = one_hot((total - low, cap), low - len0)
    for c, out_ref in enumerate(outs):
        first = jnp.where(m == 0, a_ref[c], b_ref[c])
        second = jnp.where(m == 0, b_ref[c], a_ref[c])
        moved = dot(pick, second)
        out_ref[:low] = first[:low]
        out_ref[low:cap] = (moved[: cap - low] + first[low:].astype(jnp.float32)).astype(out_ref.dtype)
        out_ref[cap:] = moved[cap - low :].astype(out_ref.dtype)


def merge_keys(scal, a, b, total):
    return pl.pallas_call(
        merge_keys_kernel,
        in_specs=[SMEM, pl.BlockSpec(), pl.BlockSpec()],
        out_shape=[jax.ShapeDtypeStruct((total, HEAD_DIM), a.dtype)] * a.shape[0],
        compiler_params=PARAMS,
    )(scal, a, b)


def attend_rows(q, g, keys, values, key_len, valid):
    scores = dot(q, keys, NT) * SCALING
    col = lax.broadcasted_iota(jnp.int32, (1, scores.shape[1]), 1)
    scores = jnp.where(col < key_len, scores, -1e30)
    raised = jnp.exp(scores - jnp.max(scores, axis=1, keepdims=True))
    probs = raised * (1.0 / jnp.sum(raised, axis=1, keepdims=True))
    probs_b = probs.astype(jnp.bfloat16)
    prob_grad = dot(g, values, NT)
    row_dot = jnp.sum(probs * prob_grad, axis=1, keepdims=True)
    score_grad = (probs * (prob_grad - row_dot)).astype(jnp.bfloat16)
    context = jnp.where(valid, dot(probs_b, values), 0.0).astype(jnp.bfloat16)
    query_grad = jnp.where(valid, dot(score_grad, keys) * SCALING, 0.0).astype(jnp.bfloat16)
    return context, query_grad, probs_b, score_grad


def attend_kernel(scal, xm_ref, xn_ref, kvm_ref, kvn_ref, ym_ref, yn_ref, dkvm_ref, dkvn_ref):
    columns = ((xm_ref, kvm_ref, ym_ref, dkvm_ref), (xn_ref, kvn_ref, yn_ref, dkvn_ref))
    for n, (x_ref, kv_ref, y_ref, dkv_ref) in enumerate(columns):
        probs, score_grads = [], []
        for base in range(0, x_ref.shape[1], ROWS):
            at = slice(base, base + ROWS)
            valid = lax.broadcasted_iota(jnp.int32, (ROWS, 1), 0) + base < scal[QUERY_LEN + n]
            y_ref[0, at], y_ref[1, at], probs_b, score_grad = attend_rows(
                x_ref[0, at], x_ref[1, at], kv_ref[0], kv_ref[1], scal[KEY_LEN + n], valid
            )
            probs.append(probs_b)
            score_grads.append(score_grad)
        key_grad = dot(jnp.concatenate(score_grads), x_ref[0], TN) * SCALING
        dkv_ref[0] = key_grad.astype(dkv_ref.dtype)
        dkv_ref[1] = dot(jnp.concatenate(probs), x_ref[1], TN).astype(dkv_ref.dtype)


def attend(scal, xm, xn, kvm, kvn):
    cap, keys = xm.shape[1], kvm.shape[1]
    return pl.pallas_call(
        attend_kernel,
        in_specs=[SMEM] + [pl.BlockSpec()] * 4,
        out_shape=[jax.ShapeDtypeStruct(a.shape, a.dtype) for a in (xm, xn, kvm, kvn)],
        compiler_params=PARAMS,
        cost_estimate=pl.CostEstimate(
            flops=24 * cap * keys * HEAD_DIM, bytes_accessed=5 * 2**20, transcendentals=2 * cap * keys
        ),
    )(scal, xm, xn, kvm, kvn)


def exchanged(parts, flag):
    def swap(parts):
        return lax.all_to_all(parts, "mp", split_axis=0, concat_axis=0, tiled=True)

    return lax.cond(flag, swap, lambda parts: parts, parts)


def local(
    queries,
    encoder_keys,
    encoder_values,
    context_grad,
    encoder_lengths,
    decoder_lengths,
    target_device,
):
    owners = lax.axis_size("dp")
    own = lax.axis_index("dp").astype(jnp.int32).reshape(1)
    seq_count = target_device.shape[1]
    dec_total = queries.shape[0] * lax.axis_size("mp")
    dec_cap = dec_total // seq_count
    enc_total = encoder_keys.shape[0]
    enc_cap = enc_total // seq_count
    way, around, scal, kvm, kvn = prepare(
        own, encoder_lengths.T, decoder_lengths.T, target_device.T, encoder_keys, encoder_values, owners, enc_cap
    )
    way, around = way[0], around[0]
    ways = [(RING * i + m, RING * i + n) for i in range(owners // RING) for m, n in KEY_HOPS][1:]
    last = len(KEY_HOPS) - 1
    rest = [(0, 0)] + [(j - KEY_HOPS[-1][0], j + 1 - KEY_HOPS[-1][1]) for j in range(last, RING // 2)]

    def queries_out(m, n):
        def run(xm, xn):
            xn = passed_along(xn, n)
            return xn, passed_along(xm, -m)

        return run

    def out_along(m, n, last):
        def run(scal, around, kvm, kvn, queries, context_grad):
            kvn = passed_along(kvn, -n)
            kvm = passed_along(kvm, m)
            xm, xn = pack(scal, exchanged(split(queries, context_grad), around >= 0), dec_cap)
            if last:
                xn, xm = lax.switch(around - 1, [queries_out(*r) for r in rest[1:]], xm, xn)
            return kvn, kvm, xn, xm

        return run

    kvn, kvm, xn, xm = lax.switch(
        way,
        [out_along(*w, i % len(KEY_HOPS) == last - 1) for i, w in enumerate(ways)],
        scal, around, kvm, kvn, queries, context_grad,
    )

    def queries_back(m, n):
        def run(ym, yn):
            yn = queries_along(yn, -n)
            return yn, queries_along(ym, m)

        return run

    ym, yn, kvm, kvn = attend(scal, xm, xn, kvm, kvn)
    yn, ym = lax.switch(around, [queries_back(*r) for r in rest], ym, yn)

    def back_along(m, n):
        def run(scal, around, kvm, kvn, ym, yn):
            kvn = passed_along(kvn, n)
            kvm = passed_along(kvm, -m)
            parts = merge_parts(scal, ym, yn, lax.axis_size("mp"))
            return kvn, kvm, *join(exchanged(parts, around >= 0))

        return run

    kvn, kvm, context, query_grad = lax.switch(
        way, [back_along(*w) for w in ways], scal, around, kvm, kvn, ym, yn
    )
    key_grad, value_grad = merge_keys(scal, kvm, kvn, enc_total)
    return (context, query_grad, key_grad, value_grad)


def solution(mesh):
    return jax.shard_map(
        local,
        mesh=mesh,
        in_specs=(
            P(("dp", "mp"), None),
            P("dp", "mp"),
            P("dp", "mp"),
            P(("dp", "mp"), None),
            P(),
            P(),
            P(),
        ),
        out_specs=(P(("dp", "mp"), None), P(("dp", "mp"), None), P("dp", "mp"), P("dp", "mp")),
        check_vma=False,
    )
```

```python
import functools

import jax
import jax.numpy as jnp
from jax import lax
from jax.experimental import pallas as pl
from jax.experimental.pallas import tpu as pltpu
from jax.sharding import PartitionSpec as P

HEAD_DIM = 256
SCALING = HEAD_DIM ** (-0.5)
ROWS = 256
RING = 16
KEY_HOPS = ((0, 1), (1, 2), (2, 3), (2, 2))
SMEM = pl.BlockSpec(memory_space=pltpu.SMEM)
NT = (((1,), (1,)), ((), ()))
TN = (((0,), (0,)), ((), ()))
COL, DEC_LEN, ENC_LEN, KEY_LEN, QUERY_LEN = 0, 2, 4, 6, 8
PARAMS = pltpu.CompilerParams(vmem_limit_bytes=32 * 2**20)
WIDE = pltpu.CompilerParams(vmem_limit_bytes=60 * 2**20)


def dot(a, b, dims=(((1,), (0,)), ((), ()))):
    return lax.dot_general(a, b, dims, preferred_element_type=jnp.float32)


def passed_along(block, distance):
    owners = lax.axis_size("dp")
    if distance % owners == 0:
        return block
    return lax.ppermute(block, "dp", [(i, (i + distance) % owners) for i in range(owners)])


def stay_kernel(in_ref, out_ref):
    pass


def queries_along(block, distance):
    if distance:
        return passed_along(block, distance)
    return pl.pallas_call(
        stay_kernel,
        in_specs=[pl.BlockSpec(memory_space=pl.ANY)],
        out_specs=pl.BlockSpec(memory_space=pl.ANY),
        out_shape=jax.ShapeDtypeStruct(block.shape, block.dtype),
        input_output_aliases={0: 0},
        compiler_params=PARAMS,
    )(block)


def one_hot(shape, gap):
    row = lax.broadcasted_iota(jnp.int32, shape, 0)
    col = lax.broadcasted_iota(jnp.int32, shape, 1)
    return (col - row == gap).astype(jnp.float32).astype(jnp.bfloat16)


def prepare_kernel(
    owners, own_ref, enc_ref, dec_ref, target_ref, k_hbm, v_hbm, way_ref, around_ref, out_ref, kvm_ref, kvn_ref, k_ref, v_ref, sems
):
    copies = [
        pltpu.make_async_copy(k_hbm, k_ref, sems.at[0]),
        pltpu.make_async_copy(v_hbm, v_ref, sems.at[1]),
    ]
    for copy in copies:
        copy.start()
    own = own_ref[0]
    shift0 = lax.rem(target_ref[0, 0], owners)
    m = jnp.where(lax.rem(shift0, RING) < RING // 2, 0, 1)
    shift = jnp.where(m == 0, shift0, owners - 1 - shift0)
    h = lax.rem(shift, RING)
    k = lax.div(shift, RING)
    way_ref[0] = k * len(KEY_HOPS) + jnp.minimum(h, len(KEY_HOPS) - 1) - 1
    around_ref[0] = jnp.maximum(h, len(KEY_HOPS) - 2) - (len(KEY_HOPS) - 2)
    out_ref[COL] = m
    out_ref[COL + 1] = 0

    def wrapped(i):
        return lax.rem(i + 2 * owners, owners)

    for n in range(2):
        col = m if n == 0 else 1 - m
        sign = 1 - 2 * n
        hops = KEY_HOPS[-1][n]
        for j in range(len(KEY_HOPS) - 1):
            hops = jnp.where(h == j, KEY_HOPS[j][n], hops)
        out_ref[DEC_LEN + n] = dec_ref[n, own]
        out_ref[ENC_LEN + n] = enc_ref[n, own]
        out_ref[KEY_LEN + n] = enc_ref[col, wrapped(own - sign * (RING * k + hops))]
        out_ref[QUERY_LEN + n] = dec_ref[col, wrapped(own + sign * (h + n - hops))]
    for n in range(QUERY_LEN + 2, out_ref.shape[0]):
        out_ref[n] = 0
    for copy in copies:
        copy.wait()
    cap, total = kvm_ref.shape[1], k_ref.shape[0]
    pick = one_hot((cap, total), enc_ref[0, own])
    for c, ref in enumerate((k_ref, v_ref)):
        first = ref[:cap]
        second = dot(pick, ref[...]).astype(first.dtype)
        kvm_ref[c] = jnp.where(m == 0, first, second)
        kvn_ref[c] = jnp.where(m == 0, second, first)


def prepare(own, enc, dec, target, keys, values, owners, cap):
    slot = jax.ShapeDtypeStruct((2, cap, HEAD_DIM), keys.dtype)
    return pl.pallas_call(
        functools.partial(prepare_kernel, owners),
        in_specs=[SMEM] * 4 + [pl.BlockSpec(memory_space=pl.ANY)] * 2,
        out_specs=[SMEM] * 3 + [pl.BlockSpec()] * 2,
        out_shape=[jax.ShapeDtypeStruct((size,), jnp.int32) for size in (1, 1, 16)] + [slot, slot],
        scratch_shapes=[pltpu.VMEM(keys.shape, keys.dtype)] * 2 + [pltpu.SemaphoreType.DMA((2,))],
        compiler_params=WIDE,
    )(own, enc, dec, target, keys, values)


def split_kernel(q_ref, g_ref, parts_ref):
    for j in range(parts_ref.shape[0]):
        for c, in_ref in enumerate((q_ref, g_ref)):
            parts_ref[j, c] = in_ref[:, j * HEAD_DIM : (j + 1) * HEAD_DIM]


def split(queries, grads):
    rows, width = queries.shape
    return pl.pallas_call(
        split_kernel,
        out_shape=jax.ShapeDtypeStruct((width // HEAD_DIM, 2, rows, HEAD_DIM), queries.dtype),
        compiler_params=PARAMS,
    )(queries, grads)


def join_kernel(parts_ref, *outs):
    for j in range(parts_ref.shape[0]):
        for c, out_ref in enumerate(outs):
            out_ref[:, j * HEAD_DIM : (j + 1) * HEAD_DIM] = parts_ref[j, c]


def join(parts):
    heads, count, rows, _ = parts.shape
    return pl.pallas_call(
        join_kernel,
        out_shape=[jax.ShapeDtypeStruct((rows, heads * HEAD_DIM), parts.dtype)] * count,
        compiler_params=PARAMS,
    )(parts)


def pack_kernel(scal, in_ref, xm_ref, xn_ref):
    size, count, rows, _ = in_ref.shape
    m, len0, len1 = scal[COL], scal[DEC_LEN], scal[DEC_LEN + 1]

    def part(j, _):
        base = pl.multiple_of(j * rows, rows)
        at = pl.ds(base, rows)
        pick = one_hot((rows, size * rows), len0 + base)
        at_row = lax.broadcasted_iota(jnp.int32, (rows, 1), 0) + base
        for c in range(count):
            first = in_ref[j, c]
            first = jnp.where(at_row < len0, first, jnp.zeros_like(first))
            second = dot(pick, in_ref[:, c].reshape(size * rows, HEAD_DIM))
            second = jnp.where(at_row < len1, second, 0.0).astype(first.dtype)
            xm_ref[c, at, :] = jnp.where(m == 0, first, second)
            xn_ref[c, at, :] = jnp.where(m == 0, second, first)
        return 0

    lax.fori_loop(0, xm_ref.shape[1] // rows, part, 0)


def pack(scal, parts, cap):
    slot = jax.ShapeDtypeStruct((parts.shape[1], cap, HEAD_DIM), parts.dtype)
    return pl.pallas_call(
        pack_kernel,
        in_specs=[SMEM, pl.BlockSpec()],
        out_shape=[slot, slot],
        compiler_params=PARAMS,
    )(scal, parts)


def merge_parts_kernel(scal, a_ref, b_ref, parts_ref):
    size, count, rows, _ = parts_ref.shape
    cap = a_ref.shape[1]
    m, len0 = scal[COL], scal[DEC_LEN]

    def part(j, _):
        base = j * rows
        at = pl.ds(pl.multiple_of(jnp.minimum(base, cap - rows), rows), rows)
        pick = one_hot((rows, cap), base - len0)
        for c in range(count):
            first = jnp.where(m == 0, a_ref[c, at, :], b_ref[c, at, :])
            second = jnp.where(m == 0, b_ref[c], a_ref[c])
            first = jnp.where(base < cap, first, jnp.zeros_like(first)).astype(jnp.float32)
            parts_ref[j, c] = (dot(pick, second) + first).astype(parts_ref.dtype)
        return 0

    lax.fori_loop(0, size, part, 0, unroll=2)


def merge_parts(scal, a, b, parts):
    rows = a.shape[1] * 2 // parts
    return pl.pallas_call(
        merge_parts_kernel,
        in_specs=[SMEM, pl.BlockSpec(), pl.BlockSpec()],
        out_shape=jax.ShapeDtypeStruct((parts, a.shape[0], rows, HEAD_DIM), a.dtype),
        compiler_params=PARAMS,
    )(scal, a, b)


def merge_keys_kernel(scal, a_ref, b_ref, *outs):
    cap, total = a_ref.shape[1], outs[0].shape[0]
    m, len0 = scal[COL], scal[ENC_LEN]
    low = cap // 2
    pick = one_hot((total - low, cap), low - len0)
    for c, out_ref in enumerate(outs):
        first = jnp.where(m == 0, a_ref[c], b_ref[c])
        second = jnp.where(m == 0, b_ref[c], a_ref[c])
        moved = dot(pick, second)
        out_ref[:low] = first[:low]
        out_ref[low:cap] = (moved[: cap - low] + first[low:].astype(jnp.float32)).astype(out_ref.dtype)
        out_ref[cap:] = moved[cap - low :].astype(out_ref.dtype)


def merge_keys(scal, a, b, total):
    return pl.pallas_call(
        merge_keys_kernel,
        in_specs=[SMEM, pl.BlockSpec(), pl.BlockSpec()],
        out_shape=[jax.ShapeDtypeStruct((total, HEAD_DIM), a.dtype)] * a.shape[0],
        compiler_params=PARAMS,
    )(scal, a, b)


def attend_rows(q, g, keys, values, key_len, valid):
    scores = dot(q, keys, NT) * SCALING
    col = lax.broadcasted_iota(jnp.int32, (1, scores.shape[1]), 1)
    scores = jnp.where(col < key_len, scores, -1e30)
    raised = jnp.exp(scores - jnp.max(scores, axis=1, keepdims=True))
    probs = raised * (1.0 / jnp.sum(raised, axis=1, keepdims=True))
    probs_b = probs.astype(jnp.bfloat16)
    prob_grad = dot(g, values, NT)
    row_dot = jnp.sum(probs * prob_grad, axis=1, keepdims=True)
    score_grad = (probs * (prob_grad - row_dot)).astype(jnp.bfloat16)
    context = jnp.where(valid, dot(probs_b, values), 0.0).astype(jnp.bfloat16)
    query_grad = jnp.where(valid, dot(score_grad, keys) * SCALING, 0.0).astype(jnp.bfloat16)
    return context, query_grad, probs_b, score_grad


def attend_kernel(scal, xm_ref, xn_ref, kvm_ref, kvn_ref, ym_ref, yn_ref, dkvm_ref, dkvn_ref):
    columns = ((xm_ref, kvm_ref, ym_ref, dkvm_ref), (xn_ref, kvn_ref, yn_ref, dkvn_ref))
    for n, (x_ref, kv_ref, y_ref, dkv_ref) in enumerate(columns):
        probs, score_grads = [], []
        for base in range(0, x_ref.shape[1], ROWS):
            at = slice(base, base + ROWS)
            valid = lax.broadcasted_iota(jnp.int32, (ROWS, 1), 0) + base < scal[QUERY_LEN + n]
            y_ref[0, at], y_ref[1, at], probs_b, score_grad = attend_rows(
                x_ref[0, at], x_ref[1, at], kv_ref[0], kv_ref[1], scal[KEY_LEN + n], valid
            )
            probs.append(probs_b)
            score_grads.append(score_grad)
        key_grad = dot(jnp.concatenate(score_grads), x_ref[0], TN) * SCALING
        dkv_ref[0] = key_grad.astype(dkv_ref.dtype)
        dkv_ref[1] = dot(jnp.concatenate(probs), x_ref[1], TN).astype(dkv_ref.dtype)


def attend(scal, xm, xn, kvm, kvn):
    cap, keys = xm.shape[1], kvm.shape[1]
    return pl.pallas_call(
        attend_kernel,
        in_specs=[SMEM] + [pl.BlockSpec()] * 4,
        out_shape=[jax.ShapeDtypeStruct(a.shape, a.dtype) for a in (xm, xn, kvm, kvn)],
        compiler_params=PARAMS,
        cost_estimate=pl.CostEstimate(
            flops=24 * cap * keys * HEAD_DIM, bytes_accessed=5 * 2**20, transcendentals=2 * cap * keys
        ),
    )(scal, xm, xn, kvm, kvn)


def exchanged(parts, flag):
    def swap(parts):
        return lax.all_to_all(parts, "mp", split_axis=0, concat_axis=0, tiled=True)

    return lax.cond(flag, swap, lambda parts: parts, parts)


def local(
    queries,
    encoder_keys,
    encoder_values,
    context_grad,
    encoder_lengths,
    decoder_lengths,
    target_device,
):
    owners = lax.axis_size("dp")
    own = lax.axis_index("dp").astype(jnp.int32).reshape(1)
    seq_count = target_device.shape[1]
    dec_total = queries.shape[0] * lax.axis_size("mp")
    dec_cap = dec_total // seq_count
    enc_total = encoder_keys.shape[0]
    enc_cap = enc_total // seq_count
    way, around, scal, kvm, kvn = prepare(
        own, encoder_lengths.T, decoder_lengths.T, target_device.T, encoder_keys, encoder_values, owners, enc_cap
    )
    way, around = way[0], around[0]
    ways = [(RING * i + m, RING * i + n) for i in range(owners // RING) for m, n in KEY_HOPS][1:]
    last = len(KEY_HOPS) - 1
    rest = [(0, 0)] + [(j - KEY_HOPS[-1][0], j + 1 - KEY_HOPS[-1][1]) for j in range(last, RING // 2)]

    def queries_out(m, n):
        def run(xm, xn):
            xn = passed_along(xn, n)
            return xn, passed_along(xm, -m)

        return run

    def out_along(m, n, last):
        def run(scal, around, kvm, kvn, queries, context_grad):
            kvn = passed_along(kvn, -n)
            kvm = passed_along(kvm, m)
            xm, xn = pack(scal, exchanged(split(queries, context_grad), around >= 0), dec_cap)
            if last:
                xn, xm = lax.switch(around - 1, [queries_out(*r) for r in rest[1:]], xm, xn)
            return kvn, kvm, xn, xm

        return run

    kvn, kvm, xn, xm = lax.switch(
        way,
        [out_along(*w, i % len(KEY_HOPS) == last - 1) for i, w in enumerate(ways)],
        scal, around, kvm, kvn, queries, context_grad,
    )

    def queries_back(m, n):
        def run(ym, yn):
            yn = queries_along(yn, -n)
            return yn, queries_along(ym, m)

        return run

    ym, yn, kvm, kvn = attend(scal, xm, xn, kvm, kvn)
    yn, ym = lax.switch(around, [queries_back(*r) for r in rest], ym, yn)

    def back_along(m, n):
        def run(scal, around, kvm, kvn, ym, yn):
            kvn = passed_along(kvn, n)
            kvm = passed_along(kvm, -m)
            parts = merge_parts(scal, ym, yn, lax.axis_size("mp"))
            return kvn, kvm, *join(exchanged(parts, around >= 0))

        return run

    kvn, kvm, context, query_grad = lax.switch(
        way, [back_along(*w) for w in ways], scal, around, kvm, kvn, ym, yn
    )
    key_grad, value_grad = merge_keys(scal, kvm, kvn, enc_total)
    return (context, query_grad, key_grad, value_grad)


def solution(mesh):
    return jax.shard_map(
        local,
        mesh=mesh,
        in_specs=(
            P(("dp", "mp"), None),
            P("dp", "mp"),
            P("dp", "mp"),
            P(("dp", "mp"), None),
            P(),
            P(),
            P(),
        ),
        out_specs=(P(("dp", "mp"), None), P(("dp", "mp"), None), P("dp", "mp"), P("dp", "mp")),
        check_vma=False,
    )
```
